512 devices in a mesh: flow: 128 (over y, z, core), tp: 4 (over x).
Axes of the slice: x: 4, y: 8, z: 8, core: 2. Of those that a mesh axis runs over, the one named last changes fastest.
Arguments:
- packets: bfloat16 [32768, 1024], P('flow', 'tp'), may hold values from -6 to 6
- packet_flow: int32 [32768], P('flow'), may hold values from 0 to 255, as said below
- packet_pos: int32 [32768], P('flow'), may hold values from 0 to 638, as said below
- flow_holder_rank: int32 [256], replicated, may hold values from 0 to 127, as said below
- flow_first_block: int32 [256], replicated, may hold values from 0 to 5, as said below
- w_qkv: bfloat16 [3, 1024, 1024], P(None, None, 'tp'), may hold values from -0.1875 to 0.1875
- w_out: bfloat16 [1024, 1024], P('tp'), may hold values from -0.1875 to 0.1875
- w_up: bfloat16 [1024, 2048], P(None, 'tp'), may hold values from -0.1875 to 0.1875
- w_down: bfloat16 [2048, 1024], P('tp'), may hold values from -0.125 to 0.125
- gain_first: bfloat16 [1024], P('tp'), may hold values from 0.5 to 1.5
- gain_second: bfloat16 [1024], P('tp'), may hold values from 0.5 to 1.5
- head_slopes: float32 [16], P('tp'), may hold values from 0.002 to 0.3
Outputs:
- encoded: bfloat16 [32768, 1024], P('flow', 'tp')
- context: bfloat16 [32768, 1024], P('flow', 'tp')
The draws below stay inside these ranges and needn't reach their ends.
Inputs may be any that keep to these rules, and one draw needn't show every extreme that they name: `packet_flow`: each flow has 1 to 639 packets. `packet_pos`: the packets of one flow carry the positions 0 to its length - 1, once each, rising with capture time (index of flow, then row). `flow_holder_rank`: each owner holds exactly two flows. At most 5 packets of one index of flow belong to the flows of one owner, and some index sends exactly 5 to some owner. `flow_first_block`: an owner's first flow starts at block 0 and its second right after the first flow's blocks; each flow's packets fit within its blocks of 128 slots; an owner's two flows take at most 6 blocks, and some owner takes all of them.
All inputs are finite; a program needn't handle non-finite values.
Results may differ from the reference program's by a relative error of at most 0.017.
Values may be sent and summed in bfloat16 or wider, within the bound.
A program may use at most 64 MiB of HBM per device.

```python
import math
import jax
import jax.numpy as jnp
from jax import lax

D = 1024
HEADS = 16
FF = 2048
BLOCK = 128
PKT_DEV = 256
HEAD_DIM = 64
SLOTS = 768
TOKENS = 32768
FLOW_TOTAL = 256
N_FLOW = 128
N_TP = 4


def shuffle_one(key):
    return jax.random.permutation(key, PKT_DEV)


def layout(key):
    key_class, key_cut, key_flow_index, key_time = jax.random.split(key, 4)
    owners = N_FLOW
    order = jax.random.permutation(key_class, owners).astype(jnp.int32)
    large = order % 4 == 3
    per_shard = PKT_DEV // BLOCK
    first_blocks = jnp.where(large, 4 * per_shard - 3, 1).astype(jnp.int32)
    cut = jax.random.randint(key_cut, (owners,), 1, BLOCK).astype(jnp.int32)
    cut = jnp.where(order == 3, 1, cut).astype(jnp.int32)
    first_len = first_blocks * BLOCK - cut
    owner_len = first_len + cut
    owner_end = jnp.cumsum(owner_len).astype(jnp.int32)
    owner_begin = owner_end - owner_len
    entry = jnp.arange(TOKENS, dtype=jnp.int32)
    holder_rank_lookup = jnp.sum((entry[:, None] >= owner_end[None, :]).astype(jnp.int32), axis=1).astype(jnp.int32)
    inner = entry - owner_begin[holder_rank_lookup]
    second_half = (inner >= first_len[holder_rank_lookup]).astype(jnp.int32)
    relabel_flows = jax.random.permutation(key_flow_index, FLOW_TOTAL).astype(jnp.int32)
    entry_flow_index = relabel_flows[2 * holder_rank_lookup + second_half]
    shuffles = jax.vmap(shuffle_one)(jax.random.split(key_time, owners)).astype(jnp.int32)
    source = jnp.arange(owners, dtype=jnp.int32)[:, None]
    held = (shuffles * owners + source).reshape(-1)
    packet_flow = entry_flow_index[held]
    by_flow = jnp.argsort(packet_flow, stable=True).astype(jnp.int32)
    rank = jnp.zeros((TOKENS,), jnp.int32).at[by_flow].set(entry)
    counts = jax.ops.segment_sum(jnp.ones((TOKENS,), jnp.int32), packet_flow, FLOW_TOTAL).astype(jnp.int32)
    flow_begin = jnp.cumsum(counts).astype(jnp.int32) - counts
    packet_pos = rank - flow_begin[packet_flow]
    local_index = jnp.arange(FLOW_TOTAL, dtype=jnp.int32)
    flow_holder_rank = jnp.zeros((FLOW_TOTAL,), jnp.int32).at[relabel_flows].set(local_index // 2)
    local_first_block = jnp.where(local_index % 2 == 0, 0, first_blocks[local_index // 2]).astype(jnp.int32)
    flow_first_block = jnp.zeros((FLOW_TOTAL,), jnp.int32).at[relabel_flows].set(local_first_block)
    return (packet_flow, packet_pos, flow_holder_rank, flow_first_block)


def draw_packet_flow(key, part):
    return layout(key)[0]


def draw_packet_pos(key, part):
    return layout(key)[1]


def draw_flow_holder_rank(key, part):
    return layout(key)[2]


def draw_flow_first_block(key, part):
    return layout(key)[3]


def steps_of(own_key, extent, shards, smallest, high):
    level, own = 1.0, jax.random.fold_in(own_key, 6)
    for dim, blocks in shards:
        steps = jnp.exp(jax.random.uniform(jax.random.fold_in(own, dim), (blocks,), jnp.float32, smallest / len(shards), high / len(shards)))
        level = level * jnp.repeat(steps, extent[dim] // blocks).reshape([-1 if axis == dim else 1 for axis in range(len(extent))])
    return level


def centred(own_key, shape, scale, most, shards=(), kind=jnp.bfloat16):
    values = scale * jax.random.normal(own_key, shape, jnp.float32)
    if shards:
        values = values * steps_of(own_key, shape, shards, -0.22, 0.18)
    return jnp.clip(values, -most, most).astype(kind)


def setup_inputs(seed: int = 0) -> dict:
    splits = jax.random.split(jax.random.key(seed), 13)
    packets = centred(splits[0], (TOKENS, D), 1.0, 6.0, ((0, 128), (1, 4)))
    packet_flow = draw_packet_flow(jax.random.fold_in(splits[12], 71), 0)
    packet_pos = draw_packet_pos(jax.random.fold_in(splits[12], 71), 0)
    flow_holder_rank = draw_flow_holder_rank(jax.random.fold_in(splits[12], 71), 0)
    flow_first_block = draw_flow_first_block(jax.random.fold_in(splits[12], 71), 0)
    w_qkv = centred(splits[5], (3, D, D), D ** -0.5, 0.1875, ((2, 4),))
    w_out = centred(splits[6], (D, D), D ** -0.5, 0.1875, ((0, 4),))
    w_up = centred(splits[7], (D, FF), D ** -0.5, 0.1875, ((1, 4),))
    w_down = centred(splits[8], (FF, D), FF ** -0.5, 0.125, ((0, 4),))
    gain_first = jnp.clip(1.0 + 0.1 * jax.random.normal(splits[9], (D,), jnp.float32), 0.5, 1.5).astype(jnp.bfloat16)
    gain_second = jnp.clip(1.0 + 0.1 * jax.random.normal(splits[10], (D,), jnp.float32), 0.5, 1.5).astype(jnp.bfloat16)
    head_slopes = jnp.clip(jnp.exp(math.log(0.3) - 5.0106353 * jax.random.uniform(splits[11], (HEADS,), jnp.float32) ** steps_of(splits[11], (HEADS,), ((0, 4),), -0.2, 0.2)), 0.002, 0.3)
    return dict(packets=packets, packet_flow=packet_flow, packet_pos=packet_pos, flow_holder_rank=flow_holder_rank, flow_first_block=flow_first_block, w_qkv=w_qkv, w_out=w_out, w_up=w_up, w_down=w_down, gain_first=gain_first, gain_second=gain_second, head_slopes=head_slopes)


EPS = 1e-05

def normalize(rows, gain):
    values = rows.astype(jnp.float32)
    mean = lax.optimization_barrier(jnp.sum(values, axis=1, keepdims=True)) / D
    spread = lax.optimization_barrier(jnp.sum(values * values, axis=1, keepdims=True)) / D - mean * mean
    return ((values - mean) * lax.rsqrt(spread + EPS) * gain.astype(jnp.float32)).astype(jnp.bfloat16)

def grouped(left, weight, groups):
    width = left.shape[1] // groups
    parts = left.astype(jnp.float32).reshape(left.shape[0], groups, width)
    blocks = weight.astype(jnp.float32).reshape(groups, width, weight.shape[1])
    terms = jnp.einsum('sgc,gcd->gsd', parts, blocks).astype(jnp.bfloat16)
    return lax.optimization_barrier(jnp.sum(terms.astype(jnp.float32), axis=0))

def reference(packets, packet_flow, packet_pos, flow_holder_rank, flow_first_block, w_qkv, w_out, w_up, w_down, gain_first, gain_second, head_slopes):
    owner = flow_holder_rank[packet_flow]
    start = flow_first_block[packet_flow]
    gslot = (owner * SLOTS + start * BLOCK + packet_pos).astype(jnp.int32)
    buffers = jnp.zeros((N_FLOW * SLOTS, D), jnp.bfloat16).at[gslot].set(packets).reshape(N_FLOW, SLOTS, D)
    flow_of = jnp.full((N_FLOW * SLOTS,), -1, jnp.int32).at[gslot].set(packet_flow).reshape(N_FLOW, SLOTS)
    place = jnp.arange(SLOTS, dtype=jnp.int32)
    distance = jnp.abs(place[:, None] - place[None, :]).astype(jnp.float32)
    itself = place[:, None] == place[None, :]
    scale = HEAD_DIM ** (-0.5)
    qkv_weight = w_qkv.astype(jnp.float32)

    def owner_layer(inputs):
        rows, tags = inputs
        normed = normalize(rows, gain_first)
        qkv = jnp.einsum('sd,kdc->ksc', normed.astype(jnp.float32), qkv_weight).astype(jnp.bfloat16)
        queries = qkv[0].reshape(SLOTS, HEADS, HEAD_DIM).astype(jnp.float32)
        keys = qkv[1].reshape(SLOTS, HEADS, HEAD_DIM).astype(jnp.float32)
        values = qkv[2].reshape(SLOTS, HEADS, HEAD_DIM).astype(jnp.float32)
        scores = jnp.einsum('qhd,khd->hqk', queries, keys) * scale - head_slopes[:, None, None] * distance[None]
        allowed = (tags[:, None] == tags[None, :]) & (tags[None, :] >= 0) | itself
        weights = jnp.where(allowed[None], jnp.exp(scores), 0.0)
        probs = (weights / lax.optimization_barrier(jnp.sum(weights, axis=2, keepdims=True))).astype(jnp.bfloat16)
        attended = jnp.einsum('hqk,khd->qhd', probs.astype(jnp.float32), values).astype(jnp.bfloat16).reshape(SLOTS, D)
        middle = (rows.astype(jnp.float32) + grouped(attended, w_out, N_TP)).astype(jnp.bfloat16)
        normed_second = normalize(middle, gain_second)
        active = jax.nn.gelu(jnp.dot(normed_second, w_up, preferred_element_type=jnp.float32), approximate=False).astype(jnp.bfloat16)
        return (middle.astype(jnp.float32) + grouped(active, w_down, N_TP)).astype(jnp.bfloat16)
    encoded_slots = lax.map(owner_layer, (buffers, flow_of))
    encoded = encoded_slots.reshape(N_FLOW * SLOTS, D)[gslot]
    totals = jax.ops.segment_sum(encoded.astype(jnp.float32), packet_flow, FLOW_TOTAL)
    counts = jax.ops.segment_sum(jnp.ones(packet_flow.shape, jnp.float32), packet_flow, FLOW_TOTAL)
    pooled = (totals / counts[:, None]).astype(jnp.bfloat16)
    context = pooled[packet_flow]
    return (encoded, context)
```

```python
import functools

import jax
import jax.numpy as jnp
from jax import lax
from jax.experimental import pallas as pl
from jax.experimental.pallas import tpu as pltpu
from jax.sharding import PartitionSpec as P

MESH = pl.DeviceIdType.MESH
F32, BF16 = jnp.float32, jnp.bfloat16
D = 1024
BLOCK = 128
SLOTS = 768
HEAD_DIM = 64
EPS = 1e-05
DIGIT = 128
LOG2E = 1.4426950408889634
FAR = 1e30
VMEM_LIMIT = 48 * 1024 * 1024
VMEM = pl.BlockSpec(memory_space=pltpu.VMEM)
SMEM = pl.BlockSpec(memory_space=pltpu.SMEM)


def iota(shape, dim):
    return lax.broadcasted_iota(jnp.int32, shape, dim)


def to_row(column):
    n = column.shape[0]
    eye = iota((n, n), 0) == iota((n, n), 1)
    return jnp.sum(jnp.where(eye, column, 0.0), axis=0, keepdims=True)


def to_column(row):
    n = row.shape[1]
    eye = iota((n, n), 0) == iota((n, n), 1)
    return jnp.sum(jnp.where(eye, row, 0.0), axis=1, keepdims=True)


def onehot(mask):
    return jnp.where(mask, 1.0, 0.0).astype(BF16)


def to_blocks(left, right):
    n = left.shape[0] // 8
    return jnp.concatenate([left.reshape(n, 8, 128), right.reshape(n, 8, 128)], axis=1).astype(BF16)


def from_blocks(blocks):
    n = blocks.shape[0]
    wide = blocks.astype(F32)
    return wide[:, :8].reshape(n * 8, 128).astype(BF16), wide[:, 8:].reshape(n * 8, 128).astype(BF16)


def pack_kernel(side, scal_ref, pk_ref, flow_ref, pos_ref, holder_ref, first_ref, out_ref, rows_ref):
    core, place = scal_ref[0], scal_ref[1]
    here, flows = pk_ref.shape[0], holder_ref.shape[1]
    rows = out_ref.shape[0] * 8
    flow = to_column(flow_ref[...].astype(F32)).astype(jnp.int32)
    pos = to_column(pos_ref[...].astype(F32))
    pick = flow == iota((here, flows), 1)
    dest = jnp.sum(jnp.where(pick, holder_ref[...].astype(F32), 0.0), axis=1, keepdims=True)
    first = jnp.sum(jnp.where(pick, first_ref[...].astype(F32), 0.0), axis=1, keepdims=True)
    code = first * BLOCK + pos + 1.0
    high = jnp.floor(code * (1.0 / DIGIT))
    low = code - high * DIGIT
    before = (dest == to_row(dest)) & (iota((here, here), 0) > iota((here, here), 1))
    rank = jnp.sum(jnp.where(before, 1.0, 0.0), axis=1, keepdims=True)
    owner = dest.astype(jnp.int32)
    chip = lax.shift_right_logical(owner, 1)
    major = lax.div(chip, side)
    minor = chip - major * side
    swap = core == 1
    block = 2 * (side * jnp.where(swap, minor, major) + jnp.where(swap, major, minor)) + (owner & 1)
    base = (block * 8).astype(F32)
    base_row = to_row(base)
    rank_row = to_row(rank)
    sub = iota((rows, here), 0).astype(F32)
    take = onehot(sub == base_row + rank_row)
    take_high = onehot(sub == base_row + 5.0)
    take_low = onehot(sub == base_row + 6.0)
    lane = iota((here, 128), 1).astype(F32) - ((place & 15) * 8).astype(F32)
    mine = lane == rank
    left = (
        jnp.dot(take, pk_ref[:, :128], preferred_element_type=F32)
        + jnp.dot(take_high, jnp.where(mine, high, 0.0).astype(BF16), preferred_element_type=F32)
        + jnp.dot(take_low, jnp.where(mine, low, 0.0).astype(BF16), preferred_element_type=F32)
    )
    right = jnp.dot(take, pk_ref[:, 128:], preferred_element_type=F32)
    out_ref[...] = to_blocks(left, right)
    at = iota((here, 128), 1)
    pool = base + 5.0 + jnp.where(first > 0.0, 1.0, 0.0)
    rows_ref[...] = jnp.where(at == 0, base + rank, pool)


def unpack_kernel(in_ref, gain_ref, out_ref, code_ref, fill_ref):
    blocks = in_ref.shape[0]
    rows = blocks * 8
    groups = rows // 128
    left, right = from_blocks(in_ref[...])
    r, g = iota((8, rows), 1), iota((8, rows), 0)
    group = lax.shift_right_logical(r, 7) == g
    high = jnp.dot(onehot(group & ((r & 7) == 5)), left, preferred_element_type=F32)
    low = jnp.dot(onehot(group & ((r & 7) == 6)), left, preferred_element_type=F32)
    code = high * DIGIT + low - 1.0
    code_ref[...] = code
    slot = iota((SLOTS, 128), 0).astype(F32)
    place = jnp.concatenate([onehot(slot == code[i : i + 1]) for i in range(groups)], axis=1)
    out_ref[:SLOTS, :128] = jnp.dot(place, left, preferred_element_type=F32).astype(BF16)
    out_ref[:SLOTS, 128:] = jnp.dot(place, right, preferred_element_type=F32).astype(BF16)
    out_ref[SLOTS:, :] = gain_ref[...]
    fill_ref[...] = lax.dot_general(
        jnp.ones((8, rows), BF16), place, (((1,), (1,)), ((), ())), preferred_element_type=F32
    )


def norm_parts(parts, gains):
    total = sum(jnp.sum(p, axis=1, keepdims=True) for p in parts)
    square = sum(jnp.sum(p * p, axis=1, keepdims=True) for p in parts)
    mean = total / D
    scale = lax.rsqrt(square / D - mean * mean + EPS)
    return [((p - mean) * scale * g).astype(BF16) for p, g in zip(parts, gains)]


def attend_kernel(scal_ref, slope_ref, all_ref, fill_ref, w_ref, out_ref, normed_ref, qkv_ref, far_ref):
    steps = SLOTS // BLOCK
    parts = all_ref.shape[0]
    gains = [all_ref[p, SLOTS : SLOTS + 16, :].astype(F32)[0:1] for p in range(parts)]
    width = out_ref.shape[1]
    edge = scal_ref[2] * BLOCK

    @pl.loop(0, steps)
    def _(step):
        rows = pl.ds(pl.multiple_of(step * BLOCK, BLOCK), BLOCK)
        normed = norm_parts([all_ref[p, rows, :].astype(F32) for p in range(parts)], gains)
        for p in range(parts):
            normed_ref[rows, p * width : (p + 1) * width] = normed[p]
        here = iota((BLOCK, SLOTS), 0) + step * BLOCK
        there = iota((BLOCK, SLOTS), 1)
        allowed = (((here >= edge) == (there >= edge)) & (fill_ref[0:1, :] > 0.0)) | (here == there)
        far_ref[rows, :] = jnp.where(allowed, jnp.abs(here - there).astype(F32) * LOG2E, FAR)

    for k in range(3):
        qkv_ref[k] = jnp.dot(normed_ref[...], w_ref[k], preferred_element_type=F32).astype(BF16)

    @pl.loop(0, steps)
    def _(step):
        rows = pl.ds(pl.multiple_of(step * BLOCK, BLOCK), BLOCK)
        far = far_ref[rows, :]
        first = iota((BLOCK, 128), 1) < HEAD_DIM
        for pair in range(width // 128):
            cols = slice(pair * 128, (pair + 1) * 128)
            query = qkv_ref[0, rows, cols]
            keys, values = qkv_ref[1, :, cols], qkv_ref[2, :, cols]
            halves = []
            for half in range(2):
                mine = jnp.where(first == (half == 0), query, jnp.zeros_like(query))
                scores = lax.dot_general(mine, keys, (((1,), (1,)), ((), ())), preferred_element_type=F32)
                weights = jnp.exp2(
                    scores * (HEAD_DIM**-0.5 * LOG2E) - slope_ref[2 * pair + half] * far
                )
                probs = weights * (1.0 / jnp.sum(weights, axis=1, keepdims=True))
                halves.append(jnp.dot(probs.astype(BF16), values, preferred_element_type=F32))
            out_ref[rows, cols] = jnp.where(first, halves[0], halves[1]).astype(BF16)


def mlp_kernel(scal_ref, att_ref, wo_ref, all_ref, up_ref, down_ref, mid_ref, out_ref, keep_ref):
    parts, width = att_ref.shape[0], att_ref.shape[2]
    gains = [all_ref[p, SLOTS : SLOTS + 16, :].astype(F32)[1:2] for p in range(parts)]
    tall = 256

    @pl.loop(0, SLOTS // tall)
    def _(step):
        rows = pl.ds(pl.multiple_of(step * tall, tall), tall)
        attn = sum(
            jnp.dot(att_ref[p, rows, :], wo_ref[p], preferred_element_type=F32).astype(BF16).astype(F32)
            for p in range(parts)
        )
        middle = [
            (all_ref[p, rows, :].astype(F32) + attn[:, p * width : (p + 1) * width]).astype(BF16)
            for p in range(parts)
        ]
        for p in range(parts):
            keep_ref[p, rows, :] = middle[p]
        normed = jnp.concatenate(norm_parts([m.astype(F32) for m in middle], gains), axis=1)
        upward = jnp.dot(normed, up_ref[...], preferred_element_type=F32)
        active = (0.5 * upward * (1.0 + lax.erf(upward * (0.5**0.5)))).astype(BF16)
        for p in range(parts):
            out_ref[p, rows, :] = jnp.dot(
                active, down_ref[:, p * width : (p + 1) * width], preferred_element_type=F32
            ).astype(BF16)

    mid_ref[...] = keep_ref[scal_ref[3]]


def reply_kernel(scal_ref, enc_ref, code_ref, fill_ref, out_ref):
    rows = out_ref.shape[0] * 8
    edge = scal_ref[2] * BLOCK
    encoded = enc_ref[...]
    slot = iota((128, SLOTS), 1).astype(F32)
    taken = jnp.concatenate(
        [
            jnp.dot(onehot(to_column(code_ref[i : i + 1, :]) == slot), encoded, preferred_element_type=F32)
            for i in range(rows // 128)
        ],
        axis=0,
    )
    second = iota((8, SLOTS), 1) >= edge
    members = jnp.where((fill_ref[...] > 0.0) & (second == (iota((8, SLOTS), 0) == 1)), 1.0, 0.0)
    counts = jnp.sum(members, axis=1, keepdims=True)
    pooled = jnp.dot(members.astype(BF16), encoded, preferred_element_type=F32) / counts
    width = encoded.shape[1]
    sub = iota((rows, width), 0) & 7
    full = jnp.where(sub == 5, pooled[0:1], jnp.where(sub == 6, pooled[1:2], taken))
    out_ref[...] = to_blocks(full[:, :128], full[:, 128:])


def final_kernel(in_ref, rows_ref, enc_ref, ctx_ref):
    left, right = from_blocks(in_ref[...])
    here, rows = rows_ref.shape[0], left.shape[0]
    at = iota((here, rows), 1).astype(F32)
    for column, out in ((0, enc_ref), (1, ctx_ref)):
        pick = onehot(at == rows_ref[:, column : column + 1])
        out[:, :128] = jnp.dot(pick, left, preferred_element_type=F32).astype(BF16)
        out[:, 128:] = jnp.dot(pick, right, preferred_element_type=F32).astype(BF16)


class Spot:
    def __init__(self, side):
        self.side = side
        flow = lax.axis_index("flow")
        self.tp = lax.axis_index("tp")
        self.core = lax.rem(flow, 2)
        chip = flow // 2
        self.y = chip // side
        self.z = lax.rem(chip, side)

    def seen(self, core):
        first = core == 0
        return jnp.where(first, self.y, self.z), jnp.where(first, self.z, self.y)

    def device(self, core, a, b, target_core):
        first = core == 0
        y, z = jnp.where(first, a, b), jnp.where(first, b, a)
        return ((y * self.side + z) * 2 + target_core, self.tp)

    def beside(self, step):
        parts = lax.axis_size("tp")
        return (lax.axis_index("flow"), lax.rem(self.tp + step + parts, parts))


def enter(devices, count):
    barrier = pltpu.get_barrier_semaphore()
    for device in devices:
        pl.semaphore_signal(barrier, inc=1, device_id=device, device_id_type=MESH)
    pl.semaphore_wait(barrier, count)


def remote(src, dst, send, recv, device):
    return pltpu.make_async_remote_copy(
        src_ref=src, dst_ref=dst, send_sem=send, recv_sem=recv, device_id=device, device_id_type=MESH
    )


class Ring:
    def __init__(self, spot, src, out, send, recv, cut):
        self.me = spot.tp
        self.right, self.left = spot.beside(1), spot.beside(-1)
        self.src, self.out, self.send, self.recv = src, out, send, recv
        rows = src.shape[0]
        self.upper, self.lower = pl.ds(0, cut), pl.ds(cut, rows - cut)
        parts = lax.axis_size("tp")
        self.before = lax.rem(self.me + parts - 1, parts)
        self.after = lax.rem(self.me + 1, parts)
        self.far = lax.rem(self.me + 2, parts)

    def copy(self, i, block, part, device, own=False):
        src = self.src.at[part] if own else self.out.at[block, part]
        return remote(src, self.out.at[block, part], self.send.at[i], self.recv.at[i], device)

    def start(self):
        self.first = [
            self.copy(0, self.me, self.upper, self.right, True),
            self.copy(1, self.me, self.lower, self.left, True),
            self.copy(2, self.me, self.lower, self.right, True),
            self.copy(3, self.me, self.upper, self.left, True),
        ]
        for copy in self.first:
            copy.start()

    def forward(self):
        self.copy(0, self.before, self.upper, self.right).wait_recv()
        self.up = self.copy(4, self.before, self.upper, self.right)
        self.up.start()
        self.copy(1, self.after, self.lower, self.left).wait_recv()
        self.down = self.copy(5, self.after, self.lower, self.left)
        self.down.start()

    def finish(self):
        self.copy(2, self.before, self.lower, self.right).wait_recv()
        self.copy(3, self.after, self.upper, self.left).wait_recv()
        self.copy(4, self.far, self.upper, self.right).wait_recv()
        self.copy(5, self.far, self.lower, self.left).wait_recv()
        for copy in (*self.first, self.up, self.down):
            copy.wait_send()


def send_kernel(side, in_ref, w_ref, out_ref, wall_ref, mid, s1, r1, s2, r2, s3, r3):
    spot = Spot(side)
    core = spot.core
    a, b = spot.seen(core)
    other = 1 - core
    oa, ob = spot.seen(other)

    def turn(value, i):
        return lax.rem(value + i, side)

    sources = [spot.device(core, turn(a, i), b, core) for i in range(1, side)]
    sources += [spot.device(core, a, turn(b, i), core) for i in range(1, side)]
    sources += [spot.device(other, oa, turn(ob, i), other) for i in range(side)]
    sources += [spot.beside(1), spot.beside(-1)]
    enter(sources, len(sources))

    first = []
    for i in range(1, side):
        to = turn(a, i)
        copy = remote(in_ref.at[to], mid.at[a], s1.at[i], r1.at[i], spot.device(core, to, b, core))
        copy.start()
        first.append(copy)
    ring = Ring(spot, w_ref, wall_ref, s3, r3, w_ref.shape[0] // 2)
    ring.start()
    mid[a] = in_ref[a]
    wall_ref[spot.tp] = w_ref[...]
    for i in range(1, side):
        came = turn(a, side - i)
        remote(in_ref.at[came], mid.at[came], s1.at[i], r1.at[i], spot.device(core, a, b, other)).wait_recv()
    second = []
    for i in range(side):
        to = turn(b, i)
        for t in range(2):
            target = lax.rem(core + t, 2)
            if i == 0 and t == 0:
                continue
            copy = remote(
                mid.at[:, to, target], out_ref.at[core, b], s2.at[i, t], r2.at[i, t], spot.device(core, a, to, target)
            )
            copy.start()
            second.append(copy)
    out_ref[core, b] = mid[:, b, core]
    ring.forward()
    for i in range(side):
        for t in range(2):
            if i == 0 and t == 0:
                continue
            source = core if t == 0 else other
            came = turn(b if t == 0 else ob, side - i)
            remote(
                mid.at[:, 0, 0], out_ref.at[source, came], s2.at[i, t], r2.at[i, t], spot.device(core, a, b, other)
            ).wait_recv()
    ring.finish()
    for copy in first + second:
        copy.wait_send()


def return_kernel(side, in_ref, out_ref, mid, s1, r1, s2, r2):
    spot = Spot(side)
    core = spot.core
    a, b = spot.seen(core)
    other = 1 - core
    oa, ob = spot.seen(other)

    def turn(value, i):
        return lax.rem(value + i, side)

    sources = [spot.device(core, turn(a, i), b, core) for i in range(1, side)]
    sources += [
        spot.device(core, a, turn(b, i), lax.rem(core + t, 2)) for i in range(side) for t in range(2) if i or t
    ]
    enter(sources, len(sources))

    first = []
    for i in range(side):
        for t in range(2):
            if i == 0 and t == 0:
                continue
            frame, fa, fb = (core, a, b) if t == 0 else (other, oa, ob)
            to = turn(fb, i)
            copy = remote(
                in_ref.at[frame, to], mid.at[:, fb, core], s1.at[i, t], r1.at[i, t], spot.device(frame, fa, to, frame)
            )
            copy.start()
            first.append(copy)
    mid[:, b, core] = in_ref[core, b]
    for i in range(side):
        for t in range(2):
            if i == 0 and t == 0:
                continue
            came = turn(b, side - i)
            remote(
                in_ref.at[0, 0], mid.at[:, came, lax.rem(core + t, 2)], s1.at[i, t], r1.at[i, t],
                spot.device(core, a, b, other),
            ).wait_recv()
    second = []
    for i in range(1, side):
        to = turn(a, i)
        copy = remote(mid.at[to], out_ref.at[a], s2.at[i], r2.at[i], spot.device(core, to, b, core))
        copy.start()
        second.append(copy)
    out_ref[a] = mid[a]
    for i in range(1, side):
        came = turn(a, side - i)
        remote(mid.at[came], out_ref.at[came], s2.at[i], r2.at[i], spot.device(core, a, b, other)).wait_recv()
    for copy in first + second:
        copy.wait_send()


def gather_kernel(cut, in_ref, out_ref, send, recv):
    spot = Spot(1)
    enter([spot.beside(1), spot.beside(-1)], 2)
    ring = Ring(spot, in_ref, out_ref, send, recv, cut)
    ring.start()
    out_ref[spot.tp] = in_ref[...]
    ring.forward()
    ring.finish()


def reduce_kernel(in_ref, mid_ref, out_ref, relay, pair, one, send, recv):
    spot = Spot(1)
    parts = lax.axis_size("tp")
    me = spot.tp
    right, left = spot.beside(1), spot.beside(-1)
    after, before, far = (lax.rem(me + i, parts) for i in (1, parts - 1, 2))
    half = out_ref.shape[0] // 2
    upper, lower = pl.ds(0, half), pl.ds(half, half)
    enter([right, left], 2)
    copies = [
        remote(in_ref.at[far, upper], relay.at[0], send.at[0], recv.at[0], right),
        remote(in_ref.at[far, lower], relay.at[1], send.at[1], recv.at[1], left),
        remote(in_ref.at[after, lower], one.at[1], send.at[2], recv.at[2], right),
        remote(in_ref.at[before, upper], one.at[0], send.at[3], recv.at[3], left),
    ]
    for copy in copies:
        copy.start()
    for i, (to, rows, device) in enumerate(((after, upper, right), (before, lower, left))):
        copies[i].wait_recv()
        copies[i].wait_send()
        relay[i] = (relay[i].astype(F32) + in_ref[to, rows, :].astype(F32)).astype(BF16)
        copy = remote(relay.at[i], pair.at[i], send.at[4 + i], recv.at[4 + i], device)
        copy.start()
        copies.append(copy)
    copies[2].wait_recv()
    copies[3].wait_recv()
    for i, rows in ((0, upper), (1, lower)):
        copies[4 + i].wait_recv()
        terms = in_ref[me, rows, :].astype(F32) + pair[i].astype(F32) + one[i].astype(F32)
        out_ref[rows, :] = (mid_ref[rows, :].astype(F32) + terms).astype(BF16)
    for copy in copies[2:]:
        copy.wait_send()


def shape(*dims, dtype=BF16):
    return jax.ShapeDtypeStruct(dims, dtype)


def local(kernel, outs, specs, scratch=()):
    return pl.pallas_call(
        kernel,
        out_shape=outs,
        in_specs=specs,
        out_specs=jax.tree.map(lambda _: VMEM, outs),
        scratch_shapes=list(scratch),
        compiler_params=pltpu.CompilerParams(vmem_limit_bytes=VMEM_LIMIT),
    )


def linked(kernel, outs, inputs, scratch, number):
    return pl.pallas_call(
        kernel,
        out_shape=outs,
        in_specs=[VMEM] * inputs,
        out_specs=jax.tree.map(lambda _: VMEM, outs),
        scratch_shapes=scratch,
        compiler_params=pltpu.CompilerParams(
            vmem_limit_bytes=VMEM_LIMIT, collective_id=number, has_side_effects=True
        ),
    )


def dma(*dims):
    return pltpu.SemaphoreType.DMA(dims)


def on_device(
    packets, packet_flow, packet_pos, flow_holder_rank, flow_first_block,
    w_qkv, w_out, w_up, w_down, gain_first, gain_second, head_slopes,
):
    owners, parts = lax.axis_size("flow"), lax.axis_size("tp")
    side = int(round((owners // 2) ** 0.5))
    here, width = packets.shape
    flow, tp = lax.axis_index("flow"), lax.axis_index("tp")
    core, chip = flow % 2, flow // 2
    y, z = chip // side, chip % side
    place = core * side * side + jnp.where(core == 0, z * side + y, y * side + z)
    second = jnp.max(jnp.where(flow_holder_rank == flow, flow_first_block, 0))
    scal = jnp.stack([core, place, second, tp]).astype(jnp.int32)
    gains = jnp.concatenate([gain_first[None], gain_second[None], jnp.zeros((14, width), BF16)])

    outbox, rows = local(
        functools.partial(pack_kernel, side),
        (shape(owners, 16, 128), shape(here, 128, dtype=F32)),
        [SMEM] + [VMEM] * 5,
    )(scal, packets, packet_flow[None], packet_pos[None], flow_holder_rank[None], flow_first_block[None])

    inbox, w_out_all = linked(
        functools.partial(send_kernel, side),
        (shape(2, side, side, 16, 128), shape(parts, *w_out.shape)),
        2,
        [pltpu.VMEM((side, side, 2, 16, 128), BF16), dma(side), dma(side), dma(side, 2), dma(side, 2), dma(6), dma(6)],
        1,
    )(outbox.reshape(side, side, 2, 16, 128), w_out)

    buffer, codes, filled = local(
        unpack_kernel,
        (shape(SLOTS + 16, width), shape(8, 128, dtype=F32), shape(8, SLOTS, dtype=F32)),
        [VMEM] * 2,
    )(inbox.reshape(owners, 16, 128), gains)

    whole = linked(
        functools.partial(gather_kernel, 400),
        shape(parts, SLOTS + 16, width), 1, [dma(6), dma(6)], 2,
    )(buffer)

    attended = local(
        attend_kernel,
        shape(SLOTS, width),
        [SMEM, SMEM] + [VMEM] * 3,
        [pltpu.VMEM((SLOTS, D), BF16), pltpu.VMEM((3, SLOTS, width), BF16), pltpu.VMEM((SLOTS, SLOTS), F32)],
    )(scal, head_slopes, whole, filled, w_qkv)

    attended_all = linked(
        functools.partial(gather_kernel, 384),
        shape(parts, SLOTS, width), 1, [dma(6), dma(6)], 3,
    )(attended)

    middle, terms = local(
        mlp_kernel,
        (shape(SLOTS, width), shape(parts, SLOTS, width)),
        [SMEM] + [VMEM] * 5,
        [pltpu.VMEM((parts, SLOTS, width), BF16)],
    )(scal, attended_all, w_out_all, whole, w_up, w_down)

    half = pltpu.VMEM((2, SLOTS // 2, width), BF16)
    encoded = linked(reduce_kernel, shape(SLOTS, width), 2, [half, half, half, dma(6), dma(6)], 4)(terms, middle)

    reply = local(reply_kernel, shape(owners, 16, 128), [SMEM] + [VMEM] * 3)(scal, encoded, codes, filled)

    back = linked(
        functools.partial(return_kernel, side),
        shape(side, side, 2, 16, 128),
        1,
        [pltpu.VMEM((side, side, 2, 16, 128), BF16), dma(side, 2), dma(side, 2), dma(side), dma(side)],
        5,
    )(reply.reshape(2, side, side, 16, 128))

    return local(final_kernel, (shape(here, width), shape(here, width)), [VMEM] * 2)(
        back.reshape(owners, 16, 128), rows
    )


def solution(mesh):
    return jax.shard_map(
        on_device,
        mesh=mesh,
        in_specs=(
            P("flow", "tp"),
            P("flow"),
            P("flow"),
            P(),
            P(),
            P(None, None, "tp"),
            P("tp", None),
            P(None, "tp"),
            P("tp", None),
            P("tp"),
            P("tp"),
            P("tp"),
        ),
        out_specs=(P("flow", "tp"), P("flow", "tp")),
        check_vma=False,
    )
```

```python
import functools

import jax
import jax.numpy as jnp
from jax import lax
from jax.experimental import pallas as pl
from jax.experimental.pallas import tpu as pltpu
from jax.sharding import PartitionSpec as P

MESH = pl.DeviceIdType.MESH
F32, BF16 = jnp.float32, jnp.bfloat16
D = 1024
BLOCK = 128
SLOTS = 768
HEAD_DIM = 64
EPS = 1e-05
DIGIT = 128
LOG2E = 1.4426950408889634
FAR = 1e30
TALL = 256
VMEM_LIMIT = 48 * 1024 * 1024
VMEM = pl.BlockSpec(memory_space=pltpu.VMEM)
SMEM = pl.BlockSpec(memory_space=pltpu.SMEM)
HBM = pl.BlockSpec(memory_space=pltpu.HBM)


def iota(shape, dim):
    return lax.broadcasted_iota(jnp.int32, shape, dim)


def to_row(column):
    n = column.shape[0]
    eye = iota((n, n), 0) == iota((n, n), 1)
    return jnp.sum(jnp.where(eye, column, 0.0), axis=0, keepdims=True)


def to_column(row):
    n = row.shape[1]
    eye = iota((n, n), 0) == iota((n, n), 1)
    return jnp.sum(jnp.where(eye, row, 0.0), axis=1, keepdims=True)


def onehot(mask):
    return jnp.where(mask, 1.0, 0.0).astype(BF16)


def to_blocks(left, right):
    n = left.shape[0] // 8
    return jnp.concatenate([left.reshape(n, 8, 128), right.reshape(n, 8, 128)], axis=1).astype(BF16)


def from_blocks(blocks):
    n = blocks.shape[0]
    wide = blocks.astype(F32)
    return wide[:, :8].reshape(n * 8, 128).astype(BF16), wide[:, 8:].reshape(n * 8, 128).astype(BF16)


def pack_kernel(side, *refs):
    sources, (out_ref, rows_ref, edge_ref), holds, sem = refs[:5], refs[5:8], refs[8:13], refs[13]
    copies = [pltpu.make_async_copy(s, h, sem.at[i]) for i, (s, h) in enumerate(zip(sources, holds))]
    for copy in copies:
        copy.start()
    for copy in copies:
        copy.wait()
    pk_ref = holds[0]
    flow_row, pos_row, holder, first_block = (ref[...].astype(F32)[None] for ref in holds[1:])
    me = lax.axis_index("flow")
    core = lax.rem(me, 2)
    mine_major, mine_minor = lax.div(lax.div(me, 2), side), lax.rem(lax.div(me, 2), side)
    place = core * side * side + jnp.where(core == 0, mine_minor * side + mine_major, mine_major * side + mine_minor)
    here, flows = pk_ref.shape[0], holder.shape[1]
    rows = out_ref.shape[0] * 8
    second = jnp.max(jnp.where(holder == me.astype(F32), first_block, 0.0), axis=1, keepdims=True)
    edge_ref[...] = jnp.broadcast_to(second * BLOCK, edge_ref.shape)
    flow = to_column(flow_row).astype(jnp.int32)
    pos = to_column(pos_row)
    pick = flow == iota((here, flows), 1)
    dest = jnp.sum(jnp.where(pick, holder, 0.0), axis=1, keepdims=True)
    first = jnp.sum(jnp.where(pick, first_block, 0.0), axis=1, keepdims=True)
    code = first * BLOCK + pos + 1.0
    high = jnp.floor(code * (1.0 / DIGIT))
    low = code - high * DIGIT
    before = (dest == to_row(dest)) & (iota((here, here), 0) > iota((here, here), 1))
    rank = jnp.sum(jnp.where(before, 1.0, 0.0), axis=1, keepdims=True)
    owner = dest.astype(jnp.int32)
    chip = lax.shift_right_logical(owner, 1)
    major = lax.div(chip, side)
    minor = chip - major * side
    swap = core == 1
    block = 2 * (side * jnp.where(swap, minor, major) + jnp.where(swap, major, minor)) + (owner & 1)
    base = (block * 8).astype(F32)
    base_row = to_row(base)
    rank_row = to_row(rank)
    sub = iota((rows, here), 0).astype(F32)
    take = onehot(sub == base_row + rank_row)
    take_high = onehot(sub == base_row + 5.0)
    take_low = onehot(sub == base_row + 6.0)
    lane = iota((here, 128), 1).astype(F32) - ((place & 15) * 8).astype(F32)
    mine = lane == rank
    left = (
        jnp.dot(take, pk_ref[:, :128], preferred_element_type=F32)
        + jnp.dot(take_high, jnp.where(mine, high, 0.0).astype(BF16), preferred_element_type=F32)
        + jnp.dot(take_low, jnp.where(mine, low, 0.0).astype(BF16), preferred_element_type=F32)
    )
    right = jnp.dot(take, pk_ref[:, 128:], preferred_element_type=F32)
    out_ref[...] = to_blocks(left, right)
    at = iota((here, 128), 1)
    pool = base + 5.0 + jnp.where(first > 0.0, 1.0, 0.0)
    rows_ref[...] = jnp.where(at == 0, base + rank, pool)


def unpack_kernel(in_ref, gain1_ref, gain2_ref, out_ref, code_ref, fill_ref):
    blocks = in_ref.shape[0]
    rows = blocks * 8
    groups = rows // 128
    left, right = from_blocks(in_ref[...])
    r, g = iota((8, rows), 1), iota((8, rows), 0)
    group = lax.shift_right_logical(r, 7) == g
    high = jnp.dot(onehot(group & ((r & 7) == 5)), left, preferred_element_type=F32)
    low = jnp.dot(onehot(group & ((r & 7) == 6)), left, preferred_element_type=F32)
    code = high * DIGIT + low - 1.0
    code_ref[...] = code
    slot = iota((SLOTS, 128), 0).astype(F32)
    place = jnp.concatenate([onehot(slot == code[i : i + 1]) for i in range(groups)], axis=1)
    out_ref[:SLOTS, :128] = jnp.dot(place, left, preferred_element_type=F32).astype(BF16)
    out_ref[:SLOTS, 128:] = jnp.dot(place, right, preferred_element_type=F32).astype(BF16)
    one, two = gain1_ref[...].astype(F32)[None], gain2_ref[...].astype(F32)[None]
    out_ref[SLOTS:, :] = jnp.where(iota((16, out_ref.shape[1]), 0) == 0, one, two).astype(BF16)
    fill_ref[...] = lax.dot_general(
        jnp.ones((8, rows), BF16), place, (((1,), (1,)), ((), ())), preferred_element_type=F32
    )


def norm_parts(parts, gains):
    total = sum(jnp.sum(p, axis=1, keepdims=True) for p in parts)
    square = sum(jnp.sum(p * p, axis=1, keepdims=True) for p in parts)
    mean = total / D
    scale = lax.rsqrt(square / D - mean * mean + EPS)
    return [((p - mean) * scale * g).astype(BF16) for p, g in zip(parts, gains)]


def reply_kernel(edge_ref, enc_ref, code_ref, fill_ref, out_ref):
    rows = out_ref.shape[0] * 8
    edge = edge_ref[0:1, 0:1]
    encoded = enc_ref[...]
    slot = iota((128, SLOTS), 1).astype(F32)
    taken = jnp.concatenate(
        [
            jnp.dot(onehot(to_column(code_ref[i : i + 1, :]) == slot), encoded, preferred_element_type=F32)
            for i in range(rows // 128)
        ],
        axis=0,
    )
    second = iota((8, SLOTS), 1).astype(F32) >= edge
    members = jnp.where((fill_ref[...] > 0.0) & (second == (iota((8, SLOTS), 0) == 1)), 1.0, 0.0)
    counts = jnp.sum(members, axis=1, keepdims=True)
    pooled = jnp.dot(members.astype(BF16), encoded, preferred_element_type=F32) / counts
    width = encoded.shape[1]
    sub = iota((rows, width), 0) & 7
    full = jnp.where(sub == 5, pooled[0:1], jnp.where(sub == 6, pooled[1:2], taken))
    out_ref[...] = to_blocks(full[:, :128], full[:, 128:])


def final_kernel(in_ref, rows_ref, enc_ref, ctx_ref):
    left, right = from_blocks(in_ref[...])
    here, rows = rows_ref.shape[0], left.shape[0]
    at = iota((here, rows), 1).astype(F32)
    for column, out in ((0, enc_ref), (1, ctx_ref)):
        pick = onehot(at == rows_ref[:, column : column + 1])
        out[:, :128] = jnp.dot(pick, left, preferred_element_type=F32).astype(BF16)
        out[:, 128:] = jnp.dot(pick, right, preferred_element_type=F32).astype(BF16)


class Spot:
    def __init__(self, side):
        self.side = side
        flow = lax.axis_index("flow")
        self.tp = lax.axis_index("tp")
        self.core = lax.rem(flow, 2)
        chip = flow // 2
        self.y = chip // side
        self.z = lax.rem(chip, side)

    def seen(self, core):
        first = core == 0
        return jnp.where(first, self.y, self.z), jnp.where(first, self.z, self.y)

    def device(self, core, a, b, target_core):
        first = core == 0
        y, z = jnp.where(first, a, b), jnp.where(first, b, a)
        return ((y * self.side + z) * 2 + target_core, self.tp)

    def beside(self, step):
        parts = lax.axis_size("tp")
        return (lax.axis_index("flow"), lax.rem(self.tp + step + parts, parts))


def enter(devices, count):
    barrier = pltpu.get_barrier_semaphore()
    for device in devices:
        pl.semaphore_signal(barrier, inc=1, device_id=device, device_id_type=MESH)
    pl.semaphore_wait(barrier, count)


def remote(src, dst, send, recv, device):
    return pltpu.make_async_remote_copy(
        src_ref=src, dst_ref=dst, send_sem=send, recv_sem=recv, device_id=device, device_id_type=MESH
    )


class Ring:
    def __init__(self, spot, src, out, send, recv, cut, start=0, rows=None):
        self.me = spot.tp
        self.right, self.left = spot.beside(1), spot.beside(-1)
        self.src, self.out, self.send, self.recv = src, out, send, recv
        rows = src.shape[0] if rows is None else rows
        self.upper, self.lower = pl.ds(start, cut), pl.ds(start + cut, rows - cut)
        parts = lax.axis_size("tp")
        self.before = lax.rem(self.me + parts - 1, parts)
        self.after = lax.rem(self.me + 1, parts)
        self.far = lax.rem(self.me + 2, parts)

    def copy(self, i, block, part, device, own=False):
        src = self.src.at[part] if own and self.src is not None else self.out.at[block, part]
        return remote(src, self.out.at[block, part], self.send.at[i], self.recv.at[i], device)

    def start(self):
        self.first = [
            self.copy(0, self.me, self.upper, self.right, True),
            self.copy(1, self.me, self.lower, self.left, True),
            self.copy(2, self.me, self.lower, self.right, True),
            self.copy(3, self.me, self.upper, self.left, True),
        ]
        for copy in self.first:
            copy.start()

    def forward(self):
        self.copy(0, self.before, self.upper, self.right).wait_recv()
        self.up = self.copy(4, self.before, self.upper, self.right)
        self.up.start()
        self.copy(1, self.after, self.lower, self.left).wait_recv()
        self.down = self.copy(5, self.after, self.lower, self.left)
        self.down.start()

    def finish(self):
        self.copy(2, self.before, self.lower, self.right).wait_recv()
        self.copy(3, self.after, self.upper, self.left).wait_recv()
        self.copy(4, self.far, self.upper, self.right).wait_recv()
        self.copy(5, self.far, self.lower, self.left).wait_recv()
        for copy in (*self.first, self.up, self.down):
            copy.wait_send()


def send_kernel(side, in_ref, w_ref, out_ref, wall_ref, mid, s1, r1, s2, r2, s3, r3):
    spot = Spot(side)
    core = spot.core
    a, b = spot.seen(core)
    other = 1 - core
    oa, ob = spot.seen(other)

    def turn(value, i):
        return lax.rem(value + i, side)

    sources = [spot.device(core, turn(a, i), b, core) for i in range(1, side)]
    sources += [spot.device(core, a, turn(b, i), core) for i in range(1, side)]
    sources += [spot.device(other, oa, turn(ob, i), other) for i in range(side)]
    sources += [spot.beside(1), spot.beside(-1)]
    enter(sources, len(sources))

    first = []
    for i in range(1, side):
        to = turn(a, i)
        copy = remote(in_ref.at[to], mid.at[a], s1.at[i], r1.at[i], spot.device(core, to, b, core))
        copy.start()
        first.append(copy)
    ring = Ring(spot, w_ref, wall_ref, s3, r3, w_ref.shape[0] // 2)
    ring.start()
    mid[a] = in_ref[a]
    wall_ref[spot.tp] = w_ref[...]
    for i in range(1, side):
        came = turn(a, side - i)
        remote(in_ref.at[came], mid.at[came], s1.at[i], r1.at[i], spot.device(core, a, b, other)).wait_recv()
    second = []
    for i in range(side):
        to = turn(b, i)
        for t in range(2):
            target = lax.rem(core + t, 2)
            if i == 0 and t == 0:
                continue
            copy = remote(
                mid.at[:, to, target], out_ref.at[core, b], s2.at[i, t], r2.at[i, t], spot.device(core, a, to, target)
            )
            copy.start()
            second.append(copy)
    out_ref[core, b] = mid[:, b, core]
    ring.forward()
    for i in range(side):
        for t in range(2):
            if i == 0 and t == 0:
                continue
            source = core if t == 0 else other
            came = turn(b if t == 0 else ob, side - i)
            remote(
                mid.at[:, 0, 0], out_ref.at[source, came], s2.at[i, t], r2.at[i, t], spot.device(core, a, b, other)
            ).wait_recv()
    ring.finish()
    for copy in first + second:
        copy.wait_send()


def return_kernel(side, in_ref, out_ref, mid, s1, r1, s2, r2):
    spot = Spot(side)
    core = spot.core
    a, b = spot.seen(core)
    other = 1 - core
    oa, ob = spot.seen(other)

    def turn(value, i):
        return lax.rem(value + i, side)

    sources = [spot.device(core, turn(a, i), b, core) for i in range(1, side)]
    sources += [
        spot.device(core, a, turn(b, i), lax.rem(core + t, 2)) for i in range(side) for t in range(2) if i or t
    ]
    enter(sources, len(sources))

    first = []
    for i in range(side):
        for t in range(2):
            if i == 0 and t == 0:
                continue
            frame, fa, fb = (core, a, b) if t == 0 else (other, oa, ob)
            to = turn(fb, i)
            copy = remote(
                in_ref.at[frame, to], mid.at[:, fb, core], s1.at[i, t], r1.at[i, t], spot.device(frame, fa, to, frame)
            )
            copy.start()
            first.append(copy)
    mid[:, b, core] = in_ref[core, b]
    for i in range(side):
        for t in range(2):
            if i == 0 and t == 0:
                continue
            came = turn(b, side - i)
            remote(
                in_ref.at[0, 0], mid.at[:, came, lax.rem(core + t, 2)], s1.at[i, t], r1.at[i, t],
                spot.device(core, a, b, other),
            ).wait_recv()
    second = []
    for i in range(1, side):
        to = turn(a, i)
        copy = remote(mid.at[to], out_ref.at[a], s2.at[i], r2.at[i], spot.device(core, to, b, core))
        copy.start()
        second.append(copy)
    out_ref[a] = mid[a]
    for i in range(1, side):
        came = turn(a, side - i)
        remote(mid.at[came], out_ref.at[came], s2.at[i], r2.at[i], spot.device(core, a, b, other)).wait_recv()
    for copy in first + second:
        copy.wait_send()


def gather_kernel(cut, in_ref, out_ref, send, recv):
    spot = Spot(1)
    enter([spot.beside(1), spot.beside(-1)], 2)
    ring = Ring(spot, in_ref, out_ref, send, recv, cut)
    ring.start()
    out_ref[spot.tp] = in_ref[...]
    ring.forward()
    ring.finish()


class Sum:
    def __init__(self, spot, terms, relay, pair, one, send, recv, start, rows):
        parts = lax.axis_size("tp")
        self.me = spot.tp
        self.right, self.left = spot.beside(1), spot.beside(-1)
        self.after, self.before, self.far = (lax.rem(self.me + i, parts) for i in (1, parts - 1, 2))
        self.terms, self.relay, self.pair, self.one = terms, relay, pair, one
        self.send, self.recv = send, recv
        self.upper, self.lower = pl.ds(start, rows // 2), pl.ds(start + rows // 2, rows // 2)

    def copy(self, i, src, dst, device):
        copy = remote(src, dst, self.send.at[i], self.recv.at[i], device)
        copy.start()
        return copy

    def start(self):
        terms = self.terms
        self.copies = [
            self.copy(0, terms.at[self.far, self.upper], self.relay.at[0], self.right),
            self.copy(1, terms.at[self.far, self.lower], self.relay.at[1], self.left),
            self.copy(2, terms.at[self.after, self.lower], self.one.at[1], self.right),
            self.copy(3, terms.at[self.before, self.upper], self.one.at[0], self.left),
        ]

    def forward(self):
        for i, (to, rows, device) in enumerate(
            ((self.after, self.upper, self.right), (self.before, self.lower, self.left))
        ):
            self.copies[i].wait_recv()
            self.relay[i] = (self.relay[i].astype(F32) + self.terms[to, rows, :].astype(F32)).astype(BF16)
            self.copies.append(self.copy(4 + i, self.relay.at[i], self.pair.at[i], device))

    def finish(self, keep, out):
        for i in range(2, 6):
            self.copies[i].wait_recv()
        for i, rows in ((0, self.upper), (1, self.lower)):
            terms = self.terms[self.me, rows, :].astype(F32) + self.pair[i].astype(F32) + self.one[i].astype(F32)
            out[rows, :] = (keep[self.me, rows, :].astype(F32) + terms).astype(BF16)
        for copy in self.copies:
            copy.wait_send()


def core_kernel(
    slope_ref, edge_ref, all_ref, fill_ref, wq_any, wo_any, up_any, down_any, out_ref,
    normed_ref, qkv_ref, far_ref, att_ref, keep_ref, terms_ref, relay, pair, one,
    wq_ref, wo_ref, up_ref, down_ref, wsem, gsend, grecv, ssend, srecv,
):
    spot = Spot(1)
    barrier = pltpu.get_barrier_semaphore()
    for device in (spot.beside(1), spot.beside(-1)):
        pl.semaphore_signal(barrier, inc=1, device_id=device, device_id_type=MESH)
    loads = [
        pltpu.make_async_copy(src, dst, wsem.at[i])
        for i, (src, dst) in enumerate(
            ((wq_any, wq_ref), (wo_any, wo_ref), (up_any, up_ref), (down_any, down_ref))
        )
    ]
    for load in loads:
        load.start()
    parts, width = att_ref.shape[0], att_ref.shape[2]
    me = spot.tp
    chunks = SLOTS // TALL
    gains = [all_ref[p, SLOTS : SLOTS + 16, :].astype(F32) for p in range(parts)]
    edge = edge_ref[0:1, 0:1]

    @pl.loop(0, SLOTS // BLOCK)
    def _(step):
        rows = pl.ds(pl.multiple_of(step * BLOCK, BLOCK), BLOCK)
        normed = norm_parts([all_ref[p, rows, :].astype(F32) for p in range(parts)], [g[0:1] for g in gains])
        for p in range(parts):
            normed_ref[rows, p * width : (p + 1) * width] = normed[p]

    loads[0].wait()
    for k in range(3):
        qkv_ref[k] = jnp.dot(normed_ref[...], wq_ref[k], preferred_element_type=F32).astype(BF16)

    def attend(chunk):
        rows = pl.ds(chunk * TALL, TALL)
        here = (iota((TALL, SLOTS), 0) + chunk * TALL).astype(F32)
        there = iota((TALL, SLOTS), 1).astype(F32)
        allowed = (((here >= edge) == (there >= edge)) & (fill_ref[0:1, :] > 0.0)) | (here == there)
        far_ref[...] = jnp.where(allowed, jnp.abs(here - there) * LOG2E, FAR)
        first = iota((TALL, 128), 1) < HEAD_DIM
        for two in range(width // 128):
            cols = slice(two * 128, (two + 1) * 128)
            query = qkv_ref[0, rows, cols]
            keys, values = qkv_ref[1, :, cols], qkv_ref[2, :, cols]
            halves = []
            for half in range(2):
                mine = jnp.where(first == (half == 0), query, jnp.zeros_like(query))
                scores = lax.dot_general(mine, keys, (((1,), (1,)), ((), ())), preferred_element_type=F32)
                weights = jnp.exp2(
                    scores * (HEAD_DIM**-0.5 * LOG2E) - slope_ref[2 * two + half] * far_ref[...]
                )
                probs = weights * (1.0 / jnp.sum(weights, axis=1, keepdims=True))
                halves.append(jnp.dot(probs.astype(BF16), values, preferred_element_type=F32))
            att_ref[me, rows, cols] = jnp.where(first, halves[0], halves[1]).astype(BF16)

    def forward_layer(chunk):
        rows = pl.ds(chunk * TALL, TALL)
        attn = sum(
            jnp.dot(att_ref[p, rows, :], wo_ref[p], preferred_element_type=F32).astype(BF16).astype(F32)
            for p in range(parts)
        )
        middle = [
            (all_ref[p, rows, :].astype(F32) + attn[:, p * width : (p + 1) * width]).astype(BF16)
            for p in range(parts)
        ]
        for p in range(parts):
            keep_ref[p, rows, :] = middle[p]
        normed = jnp.concatenate(norm_parts([m.astype(F32) for m in middle], [g[1:2] for g in gains]), axis=1)
        upward = jnp.dot(normed, up_ref[...], preferred_element_type=F32)
        active = (0.5 * upward * (1.0 + lax.erf(upward * (0.5**0.5)))).astype(BF16)
        for p in range(parts):
            terms_ref[p, rows, :] = jnp.dot(
                active, down_ref[:, p * width : (p + 1) * width], preferred_element_type=F32
            ).astype(BF16)

    rings = [
        Ring(spot, None, att_ref, gsend.at[c], grecv.at[c], TALL // 2, c * TALL, TALL) for c in range(chunks)
    ]
    sums = [
        Sum(spot, terms_ref, relay.at[c], pair.at[c], one.at[c], ssend.at[c], srecv.at[c], c * TALL, TALL)
        for c in range(chunks)
    ]
    for c in range(chunks):
        attend(c)
        if c == 0:
            pl.semaphore_wait(barrier, 2)
        rings[c].start()
        if c:
            rings[c - 1].forward()
    for load in loads[1:]:
        load.wait()
    for c in range(chunks):
        if c == 1:
            rings[chunks - 1].forward()
        rings[c].finish()
        forward_layer(c)
        sums[c].start()
        if c:
            sums[c - 1].forward()
    sums[chunks - 1].forward()
    for c in range(chunks):
        sums[c].finish(keep_ref, out_ref)


def shape(*dims, dtype=BF16):
    return jax.ShapeDtypeStruct(dims, dtype)


def local(kernel, outs, specs, scratch=()):
    return pl.pallas_call(
        kernel,
        out_shape=outs,
        in_specs=specs,
        out_specs=jax.tree.map(lambda _: VMEM, outs),
        scratch_shapes=list(scratch),
        compiler_params=pltpu.CompilerParams(vmem_limit_bytes=VMEM_LIMIT),
    )


def linked(kernel, outs, inputs, scratch, number):
    return pl.pallas_call(
        kernel,
        out_shape=outs,
        in_specs=[VMEM] * inputs if isinstance(inputs, int) else inputs,
        out_specs=jax.tree.map(lambda _: VMEM, outs),
        scratch_shapes=scratch,
        compiler_params=pltpu.CompilerParams(
            vmem_limit_bytes=VMEM_LIMIT, collective_id=number, has_side_effects=True
        ),
    )


def dma(*dims):
    return pltpu.SemaphoreType.DMA(dims)


def on_device(
    packets, packet_flow, packet_pos, flow_holder_rank, flow_first_block,
    w_qkv, w_out, w_up, w_down, gain_first, gain_second, head_slopes,
):
    owners, parts = lax.axis_size("flow"), lax.axis_size("tp")
    side = int(round((owners // 2) ** 0.5))
    here, width = packets.shape
    given = (packets, packet_flow, packet_pos, flow_holder_rank, flow_first_block)

    outbox, rows, edge = local(
        functools.partial(pack_kernel, side),
        (shape(owners, 16, 128), shape(here, 128, dtype=F32), shape(8, 128, dtype=F32)),
        [HBM] * 5,
        [pltpu.VMEM(v.shape, v.dtype) for v in given] + [dma(5)],
    )(*given)

    inbox, w_out_all = linked(
        functools.partial(send_kernel, side),
        (shape(2, side, side, 16, 128), shape(parts, *w_out.shape)),
        2,
        [pltpu.VMEM((side, side, 2, 16, 128), BF16), dma(side), dma(side), dma(side, 2), dma(side, 2), dma(6), dma(6)],
        1,
    )(outbox.reshape(side, side, 2, 16, 128), w_out)

    buffer, codes, filled = local(
        unpack_kernel,
        (shape(SLOTS + 16, width), shape(8, 128, dtype=F32), shape(8, SLOTS, dtype=F32)),
        [VMEM] * 3,
    )(inbox.reshape(owners, 16, 128), gain_first, gain_second)

    whole = linked(
        functools.partial(gather_kernel, 400),
        shape(parts, SLOTS + 16, width), 1, [dma(6), dma(6)], 2,
    )(buffer)

    chunks, half = SLOTS // TALL, TALL // 2
    some = pltpu.VMEM((chunks, 2, half, width), BF16)
    full = pltpu.VMEM((parts, SLOTS, width), BF16)
    encoded = linked(
        core_kernel,
        shape(SLOTS, width),
        [SMEM, VMEM, VMEM, VMEM] + [HBM] * 4,
        [
            pltpu.VMEM((SLOTS, D), BF16), pltpu.VMEM((3, SLOTS, width), BF16), pltpu.VMEM((TALL, SLOTS), F32),
            full, full, full, some, some, some,
            *(pltpu.VMEM(w.shape, BF16) for w in (w_qkv, w_out_all, w_up, w_down)),
            dma(4), dma(chunks, 6), dma(chunks, 6), dma(chunks, 6), dma(chunks, 6),
        ],
        3,
    )(head_slopes, edge, whole, filled, w_qkv, w_out_all, w_up, w_down)

    reply = local(reply_kernel, shape(owners, 16, 128), [VMEM] * 4)(edge, encoded, codes, filled)

    back = linked(
        functools.partial(return_kernel, side),
        shape(side, side, 2, 16, 128),
        1,
        [pltpu.VMEM((side, side, 2, 16, 128), BF16), dma(side, 2), dma(side, 2), dma(side), dma(side)],
        5,
    )(reply.reshape(2, side, side, 16, 128))

    return local(final_kernel, (shape(here, width), shape(here, width)), [VMEM] * 2)(
        back.reshape(owners, 16, 128), rows
    )


def solution(mesh):
    return jax.shard_map(
        on_device,
        mesh=mesh,
        in_specs=(
            P("flow", "tp"),
            P("flow"),
            P("flow"),
            P(),
            P(),
            P(None, None, "tp"),
            P("tp", None),
            P(None, "tp"),
            P("tp", None),
            P("tp"),
            P("tp"),
            P("tp"),
        ),
        out_specs=(P("flow", "tp"), P("flow", "tp")),
        check_vma=False,
    )
```

```python
import functools

import jax
import jax.numpy as jnp
from jax import lax
from jax.experimental import pallas as pl
from jax.experimental.pallas import tpu as pltpu
from jax.sharding import PartitionSpec as P

MESH = pl.DeviceIdType.MESH
F32, BF16 = jnp.float32, jnp.bfloat16
D = 1024
BLOCK = 128
KEEP = 5
HEAD_ROWS = 16
HEAD_DIM = 64
EPS = 1e-05
DIGIT = 128
LOG2E = 1.4426950408889634
FAR = 1e30
TALL = 160
VMEM_LIMIT = 56 * 1024 * 1024
VMEM = pl.BlockSpec(memory_space=pltpu.VMEM)
SMEM = pl.BlockSpec(memory_space=pltpu.SMEM)
HBM = pl.BlockSpec(memory_space=pltpu.HBM)


def iota(shape, dim):
    return lax.broadcasted_iota(jnp.int32, shape, dim)


def to_row(column):
    n = column.shape[0]
    eye = iota((n, n), 0) == iota((n, n), 1)
    return jnp.sum(jnp.where(eye, column, 0.0), axis=0, keepdims=True)


def to_column(row):
    n = row.shape[1]
    eye = iota((n, n), 0) == iota((n, n), 1)
    return jnp.sum(jnp.where(eye, row, 0.0), axis=1, keepdims=True)


def onehot(mask):
    return jnp.where(mask, 1.0, 0.0).astype(BF16)


def to_blocks(left, right):
    n = left.shape[0] // 8
    return jnp.concatenate([left.reshape(n, 8, 128), right.reshape(n, 8, 128)], axis=1).astype(BF16)


def from_blocks(blocks):
    n = blocks.shape[0]
    wide = blocks.astype(F32)
    return wide[:, :8].reshape(n * 8, 128).astype(BF16), wide[:, 8:].reshape(n * 8, 128).astype(BF16)


def norm_parts(parts, gains):
    total = sum(jnp.sum(p, axis=1, keepdims=True) for p in parts)
    square = sum(jnp.sum(p * p, axis=1, keepdims=True) for p in parts)
    mean = total / D
    scale = lax.rsqrt(square / D - mean * mean + EPS)
    return [((p - mean) * scale * g).astype(BF16) for p, g in zip(parts, gains)]


def final_kernel(in_ref, rows_ref, enc_ref, ctx_ref):
    left, right = from_blocks(in_ref[...])
    here, rows = rows_ref.shape[0], left.shape[0]
    at = iota((here, rows), 1).astype(F32)
    for column, out in ((0, enc_ref), (1, ctx_ref)):
        pick = onehot(at == rows_ref[:, column : column + 1])
        out[:, :128] = jnp.dot(pick, left, preferred_element_type=F32).astype(BF16)
        out[:, 128:] = jnp.dot(pick, right, preferred_element_type=F32).astype(BF16)


class Spot:
    def __init__(self, side):
        self.side = side
        flow = lax.axis_index("flow")
        self.tp = lax.axis_index("tp")
        self.core = lax.rem(flow, 2)
        chip = lax.div(flow, 2)
        self.y = lax.div(chip, side)
        self.z = lax.rem(chip, side)

    def seen(self, core):
        first = core == 0
        return jnp.where(first, self.y, self.z), jnp.where(first, self.z, self.y)

    def device(self, core, a, b, target_core):
        first = core == 0
        a, b = lax.rem(a + self.side, self.side), lax.rem(b + self.side, self.side)
        y, z = jnp.where(first, a, b), jnp.where(first, b, a)
        return ((y * self.side + z) * 2 + target_core, self.tp)

    def beside(self, step):
        parts = lax.axis_size("tp")
        return (lax.axis_index("flow"), lax.rem(self.tp + step + parts, parts))


def remote(src, dst, send, recv, device):
    return pltpu.make_async_remote_copy(
        src_ref=src, dst_ref=dst, send_sem=send, recv_sem=recv, device_id=device, device_id_type=MESH
    )


def started(copy):
    copy.start()
    return copy


class Ring:
    def __init__(self, spot, src, out, send, recv, cut, start=0, rows=None):
        self.me = spot.tp
        self.right, self.left = spot.beside(1), spot.beside(-1)
        self.src, self.out, self.send, self.recv = src, out, send, recv
        rows = src.shape[0] if rows is None else rows
        self.upper, self.lower = pl.ds(start, cut), pl.ds(start + cut, rows - cut)
        parts = lax.axis_size("tp")
        self.before = lax.rem(self.me + parts - 1, parts)
        self.after = lax.rem(self.me + 1, parts)
        self.far = lax.rem(self.me + 2, parts)

    def copy(self, i, block, part, device, own=False):
        src = self.src.at[part] if own and self.src is not None else self.out.at[block, part]
        return remote(src, self.out.at[block, part], self.send.at[i], self.recv.at[i], device)

    def start(self):
        self.first = [
            self.copy(0, self.me, self.upper, self.right, True),
            self.copy(1, self.me, self.lower, self.left, True),
            self.copy(2, self.me, self.lower, self.right, True),
            self.copy(3, self.me, self.upper, self.left, True),
        ]
        for copy in self.first:
            copy.start()

    def forward(self):
        self.copy(0, self.before, self.upper, self.right).wait_recv()
        self.up = self.copy(4, self.before, self.upper, self.right)
        self.up.start()
        self.copy(1, self.after, self.lower, self.left).wait_recv()
        self.down = self.copy(5, self.after, self.lower, self.left)
        self.down.start()

    def finish(self):
        self.copy(2, self.before, self.lower, self.right).wait_recv()
        self.copy(3, self.after, self.upper, self.left).wait_recv()
        self.copy(4, self.far, self.upper, self.right).wait_recv()
        self.copy(5, self.far, self.lower, self.left).wait_recv()
        for copy in (*self.first, self.up, self.down):
            copy.wait_send()


class Sum:
    def __init__(self, spot, terms, relay, pair, one, send, recv, start, rows):
        parts = lax.axis_size("tp")
        self.me = spot.tp
        self.right, self.left = spot.beside(1), spot.beside(-1)
        self.after, self.before, self.far = (lax.rem(self.me + i, parts) for i in (1, parts - 1, 2))
        self.terms, self.relay, self.pair, self.one = terms, relay, pair, one
        self.send, self.recv = send, recv
        self.upper, self.lower = pl.ds(start, rows // 2), pl.ds(start + rows // 2, rows // 2)

    def copy(self, i, src, dst, device):
        copy = remote(src, dst, self.send.at[i], self.recv.at[i], device)
        copy.start()
        return copy

    def start(self):
        terms = self.terms
        self.copies = [
            self.copy(0, terms.at[self.far, self.upper], self.relay.at[0], self.right),
            self.copy(1, terms.at[self.far, self.lower], self.relay.at[1], self.left),
            self.copy(2, terms.at[self.after, self.lower], self.one.at[1], self.right),
            self.copy(3, terms.at[self.before, self.upper], self.one.at[0], self.left),
        ]

    def forward(self):
        for i, (to, rows, device) in enumerate(
            ((self.after, self.upper, self.right), (self.before, self.lower, self.left))
        ):
            self.copies[i].wait_recv()
            self.relay[i] = (self.relay[i].astype(F32) + self.terms[to, rows, :].astype(F32)).astype(BF16)
            self.copies.append(self.copy(4 + i, self.relay.at[i], self.pair.at[i], device))

    def finish(self, keep, out):
        for i in range(2, 6):
            self.copies[i].wait_recv()
        for i, rows in ((0, self.upper), (1, self.lower)):
            terms = self.terms[self.me, rows, :].astype(F32) + self.pair[i].astype(F32) + self.one[i].astype(F32)
            out[rows, :] = (keep[self.me, rows, :].astype(F32) + terms).astype(BF16)
        for copy in self.copies:
            copy.wait_send()


def pack(spot, packets, flow_row, pos_row, holder, first_block):
    side = spot.side
    a, b = spot.seen(spot.core)
    here, flows = packets.shape[0], holder.shape[1]
    rows = 2 * side * side * 8
    flow = to_column(flow_row)
    pos = to_column(pos_row)
    pick = flow == iota((here, flows), 1).astype(F32)
    dest = jnp.sum(jnp.where(pick, holder, 0.0), axis=1, keepdims=True)
    first = jnp.sum(jnp.where(pick, first_block, 0.0), axis=1, keepdims=True)
    code = first * BLOCK + pos + 1.0
    high = jnp.floor(code * (1.0 / DIGIT))
    low = code - high * DIGIT
    before = (dest == to_row(dest)) & (iota((here, here), 0) > iota((here, here), 1))
    rank = jnp.sum(jnp.where(before, 1.0, 0.0), axis=1, keepdims=True)
    chip = jnp.floor(dest * 0.5)
    half = dest - 2.0 * chip
    major = jnp.floor((chip + 0.5) * (1.0 / side))
    minor = chip - major * side
    swap = spot.core == 1

    def ahead(value, mine):
        value = value - mine.astype(F32)
        return jnp.where(value < 0.0, value + side, value)

    a_off = ahead(jnp.where(swap, minor, major), a)
    b_off = ahead(jnp.where(swap, major, minor), b)
    c_off = jnp.abs(half - spot.core.astype(F32))
    base = ((a_off * side + b_off) * 2.0 + c_off) * 8.0
    odd = b_off - 2.0 * jnp.floor(b_off * 0.5)
    spread = (odd * side + a_off) * 8.0 + rank
    base_row, rank_row = to_row(base), to_row(rank)
    sub = iota((rows, here), 0).astype(F32)
    take = onehot(sub == base_row + rank_row)
    take_high = onehot(sub == base_row + 5.0)
    take_low = onehot(sub == base_row + 6.0)
    mine = iota((here, 128), 1).astype(F32) == spread
    left = (
        jnp.dot(take, packets[:, :128], preferred_element_type=F32)
        + jnp.dot(take_high, jnp.where(mine, high, 0.0).astype(BF16), preferred_element_type=F32)
        + jnp.dot(take_low, jnp.where(mine, low, 0.0).astype(BF16), preferred_element_type=F32)
    )
    right = jnp.dot(take, packets[:, 128:], preferred_element_type=F32)
    at = iota((here, 128), 1)
    pool = base + 5.0 + jnp.where(first > 0.0, 1.0, 0.0)
    return to_blocks(left, right), jnp.where(at == 0, base + rank, pool)


def squeeze(rows, padded, turned=False):
    dims = (padded, rows) if turned else (rows, padded)
    row = iota(dims, 1 if turned else 0).astype(F32)
    place = row + (8 - KEEP) * jnp.floor((row + 0.5) * (1.0 / KEEP))
    return onehot(iota(dims, 0 if turned else 1).astype(F32) == place)


def digits(left):
    rows = left.shape[0]
    groups = rows // 128
    r, g = iota((8, rows), 1), iota((8, rows), 0)
    out = []
    for row in (5, 6):
        pick = onehot((r >= g * 128) & (r < g * 128 + 128) & ((r & 7) == row))
        found = jnp.dot(pick, left, preferred_element_type=F32)
        out.append(jnp.concatenate([found[i : i + 1] for i in range(groups)], axis=1))
    return out


def layer_kernel(
    side, slope_ref, pk_any, flow_any, pos_any, holder_any, first_any, gain1_any, gain2_any,
    wq_any, wo_any, up_any, down_any, back_ref, rows_ref,
    pk_ref, flow_ref, pos_ref, holder_ref, first_ref, gain1_ref, gain2_ref, wq_ref, up_ref, down_ref, wo_ref,
    out_box, mid_ref, in_box, rep_ref, mid2_ref,
    all_ref, qkv_ref, far_ref, att_ref, keep_ref, terms_ref, enc_ref, relay, pair, one,
    lsem, s1, r1, s2, r2, s3, r3, s4, r4, wsend, wrecv, asend, arecv, gsend, grecv, ssend, srecv,
):
    spot = Spot(side)
    core, me = spot.core, spot.tp
    other = 1 - core
    a, b = spot.seen(core)
    oa, ob = spot.seen(other)
    rounds, few = 2, side // 2

    barrier = pltpu.get_barrier_semaphore()
    friends = [spot.beside(1), spot.beside(-1), spot.device(core, a, b, other)]
    for i in range(1, side):
        friends += [
            spot.device(core, a + i, b, core), spot.device(core, a, b + i, core),
            spot.device(core, a, b + i, other), spot.device(other, oa, ob + i, other),
        ]
    for device in friends:
        pl.semaphore_signal(barrier, inc=1, device_id=device, device_id_type=MESH)

    sources = (pk_any, flow_any, pos_any, holder_any, first_any, gain1_any, gain2_any, wq_any, up_any, down_any)
    holds = (pk_ref, flow_ref, pos_ref, holder_ref, first_ref, gain1_ref, gain2_ref, wq_ref, up_ref, down_ref)
    loads = [pltpu.make_async_copy(x, h, lsem.at[i]) for i, (x, h) in enumerate(zip(sources, holds))]
    loads.append(pltpu.make_async_copy(wo_any, wo_ref.at[me], lsem.at[len(loads)]))
    for load in loads:
        load.start()
    for load in loads[:7]:
        load.wait()
    flow_row, pos_row, holder, first_block = (
        ref[...].astype(F32)[None] for ref in (flow_ref, pos_ref, holder_ref, first_ref)
    )
    mine = holder == lax.axis_index("flow").astype(F32)
    edge = jnp.max(jnp.where(mine, first_block, 0.0), axis=1, keepdims=True) * BLOCK
    blocks, found = pack(spot, pk_ref[...], flow_row, pos_row, holder, first_block)
    out_box[...] = blocks.reshape(out_box.shape)
    rows_ref[...] = found
    parts, width = all_ref.shape[0], all_ref.shape[2]
    gain_rows = jnp.where(
        iota((HEAD_ROWS, width), 0) == 0, gain1_ref[...].astype(F32)[None], gain2_ref[...].astype(F32)[None]
    ).astype(BF16)
    all_ref[me, :HEAD_ROWS, :] = gain_rows
    pl.semaphore_wait(barrier, len(friends))

    def hop1(h):
        some = pl.ds(h * few, few)
        return [
            started(
                remote(out_box.at[i, some], mid_ref.at[i, some], s1.at[h, i], r1.at[h, i],
                       spot.device(core, a + i, b, core))
            )
            for i in range(1, side)
        ]

    def hop2(h):
        return [
            started(
                remote(mid_ref.at[:, h * few + i, t], in_box.at[h, t, i], s2.at[h, i, t], r2.at[h, i, t],
                       spot.device(core, a, b + h * few + i, core if t == 0 else other))
            )
            for i in range(few) for t in range(2) if h or i or t
        ]

    first = [hop1(0)]
    weights = Ring(spot, wo_any, wo_ref, wsend, wrecv, wo_any.shape[0] // 2)
    weights.start()
    mid_ref[0] = out_box[0]
    for copy in first[0]:
        copy.wait_recv()
    second = [hop2(0)]
    first.append(hop1(1))
    in_box[0, 0, 0] = mid_ref[:, 0, 0]
    for copy in first[1]:
        copy.wait_recv()
    second.append(hop2(1))
    weights.forward()

    sources_here = side * side
    rows = sources_here * KEEP
    total = rounds * rows
    rings, high, low = [], [], []
    for h in range(rounds):
        for copy in second[h]:
            copy.wait_recv()
        left, right = from_blocks(in_box[h].reshape(sources_here, 16, 128))
        keep = squeeze(rows, sources_here * 8)
        here = pl.ds(HEAD_ROWS + h * rows, rows)
        all_ref[me, here, :128] = jnp.dot(keep, left, preferred_element_type=F32).astype(BF16)
        all_ref[me, here, 128:] = jnp.dot(keep, right, preferred_element_type=F32).astype(BF16)
        begin = HEAD_ROWS * (h > 0) + h * rows
        rings.append(
            Ring(spot, None, all_ref, asend.at[h], arecv.at[h], rows // 2, begin, rows + HEAD_ROWS * (h == 0))
        )
        rings[h].start()
        found = digits(left)
        high.append(found[0])
        low.append(found[1])
    both = jnp.where(
        iota((8, total // KEEP * 8), 0) == 0, jnp.concatenate(high, axis=1), jnp.concatenate(low, axis=1)
    ).astype(BF16)
    keep = squeeze(total, total // KEEP * 8)
    across = (((1,), (1,)), ((), ()))
    by_row = lax.dot_general(both, keep, across, preferred_element_type=F32)
    by_column = lax.dot_general(keep, both, across, preferred_element_type=F32)
    slot_row = by_row[0:1] * DIGIT + by_row[1:2] - 1.0
    slot_column = by_column[:, 0:1] * DIGIT + by_column[:, 1:2] - 1.0
    tag_row = jnp.where(slot_row >= edge, 1.0, 0.0)
    tag_column = jnp.where(slot_column >= edge, 1.0, 0.0)

    rings[0].forward()
    loads[7].wait()
    gains = None
    for h in range(rounds):
        if h + 1 < rounds:
            rings[h + 1].forward()
        rings[h].finish()
        if gains is None:
            gains = [all_ref[p, :HEAD_ROWS, :].astype(F32) for p in range(parts)]
        here = pl.ds(HEAD_ROWS + h * rows, rows)
        normed = jnp.concatenate(
            norm_parts([all_ref[p, here, :].astype(F32) for p in range(parts)], [g[0:1] for g in gains]), axis=1
        )
        for k in range(3):
            qkv_ref[k, pl.ds(h * rows, rows), :] = jnp.dot(normed, wq_ref[k], preferred_element_type=F32).astype(BF16)

    def attend(chunk):
        rows = pl.ds(chunk * TALL, TALL)
        part = slice(chunk * TALL, (chunk + 1) * TALL)
        itself = iota((TALL, total), 0) + chunk * TALL == iota((TALL, total), 1)
        allowed = ((tag_column[part] == tag_row) & (slot_row >= 0.0)) | itself
        far_ref[...] = jnp.where(allowed, jnp.abs(slot_column[part] - slot_row) * LOG2E, FAR)
        first = iota((TALL, 128), 1) < HEAD_DIM
        for two in range(width // 128):
            cols = slice(two * 128, (two + 1) * 128)
            query = qkv_ref[0, rows, cols]
            keys, values = qkv_ref[1, :, cols], qkv_ref[2, :, cols]
            halves = []
            for half in range(2):
                mine = jnp.where(first == (half == 0), query, jnp.zeros_like(query))
                scores = lax.dot_general(mine, keys, across, preferred_element_type=F32)
                weights = jnp.exp2(
                    scores * (HEAD_DIM**-0.5 * LOG2E) - slope_ref[2 * two + half] * far_ref[...]
                )
                probs = weights * (1.0 / jnp.sum(weights, axis=1, keepdims=True))
                halves.append(jnp.dot(probs.astype(BF16), values, preferred_element_type=F32))
            att_ref[me, rows, cols] = jnp.where(first, halves[0], halves[1]).astype(BF16)

    def forward_layer(chunk):
        rows = pl.ds(chunk * TALL, TALL)
        there = pl.ds(HEAD_ROWS + chunk * TALL, TALL)
        attn = sum(
            jnp.dot(att_ref[p, rows, :], wo_ref[p], preferred_element_type=F32).astype(BF16).astype(F32)
            for p in range(parts)
        )
        middle = [
            (all_ref[p, there, :].astype(F32) + attn[:, p * width : (p + 1) * width]).astype(BF16)
            for p in range(parts)
        ]
        for p in range(parts):
            keep_ref[p, rows, :] = middle[p]
        normed = jnp.concatenate(norm_parts([m.astype(F32) for m in middle], [g[1:2] for g in gains]), axis=1)
        upward = jnp.dot(normed, up_ref[...], preferred_element_type=F32)
        active = (0.5 * upward * (1.0 + lax.erf(upward * (0.5**0.5)))).astype(BF16)
        for p in range(parts):
            terms_ref[p, rows, :] = jnp.dot(
                active, down_ref[:, p * width : (p + 1) * width], preferred_element_type=F32
            ).astype(BF16)

    chunks = total // TALL
    rings = [Ring(spot, None, att_ref, gsend.at[c], grecv.at[c], TALL // 2, c * TALL, TALL) for c in range(chunks)]
    sums = [
        Sum(spot, terms_ref, relay.at[c], pair.at[c], one.at[c], ssend.at[c], srecv.at[c], c * TALL, TALL)
        for c in range(chunks)
    ]
    for c in range(chunks):
        attend(c)
        rings[c].start()
        if c:
            rings[c - 1].forward()
    weights.finish()
    for load in loads[8:]:
        load.wait()
    for c in range(chunks):
        if c == 1:
            rings[chunks - 1].forward()
        rings[c].finish()
        forward_layer(c)
        sums[c].start()
        if c:
            sums[c - 1].forward()
    sums[chunks - 1].forward()
    for c in range(chunks):
        sums[c].finish(keep_ref, enc_ref)

    encoded = enc_ref[...]
    number = iota((8, total), 0).astype(F32)
    members = jnp.where((slot_row >= 0.0) & (tag_row == number), 1.0, 0.0)
    counts = jnp.sum(members, axis=1, keepdims=True)
    pooled = jnp.dot(members.astype(BF16), encoded, preferred_element_type=F32) / counts
    wide = jnp.dot(squeeze(total, total // KEEP * 8, True), encoded, preferred_element_type=F32)
    sub = iota(wide.shape, 0) & 7
    wide = jnp.where(sub == 5, pooled[0:1], jnp.where(sub == 6, pooled[1:2], wide))
    rep_ref[...] = to_blocks(wide[:, :128], wide[:, 128:]).reshape(rep_ref.shape)

    third = []
    for h in range(rounds):
        for i in range(few):
            for t in range(2):
                if h or i or t:
                    frame, fa, fb = (core, a, b) if t == 0 else (other, oa, ob)
                    far = h * few + i
                    third.append(
                        started(
                            remote(rep_ref.at[h, t, i], mid2_ref.at[:, far, t], s3.at[far, t], r3.at[far, t],
                                   spot.device(frame, fa, fb - far, frame))
                        )
                    )
    mid2_ref[:, 0, 0] = rep_ref[0, 0, 0]
    for copy in third:
        copy.wait_recv()
    fourth = [
        started(remote(mid2_ref.at[i], back_ref.at[i], s4.at[i], r4.at[i], spot.device(core, a - i, b, core)))
        for i in range(1, side)
    ]
    back_ref[0] = mid2_ref[0]
    for copy in fourth:
        copy.wait_recv()
    for copy in (*first[0], *first[1], *second[0], *second[1], *third, *fourth):
        copy.wait_send()


def shape(*dims, dtype=BF16):
    return jax.ShapeDtypeStruct(dims, dtype)


def local(kernel, outs, specs, scratch=()):
    return pl.pallas_call(
        kernel,
        out_shape=outs,
        in_specs=specs,
        out_specs=jax.tree.map(lambda _: VMEM, outs),
        scratch_shapes=list(scratch),
        compiler_params=pltpu.CompilerParams(vmem_limit_bytes=VMEM_LIMIT),
    )


def linked(kernel, outs, inputs, scratch, number):
    return pl.pallas_call(
        kernel,
        out_shape=outs,
        in_specs=[VMEM] * inputs if isinstance(inputs, int) else inputs,
        out_specs=jax.tree.map(lambda _: VMEM, outs),
        scratch_shapes=scratch,
        compiler_params=pltpu.CompilerParams(
            vmem_limit_bytes=VMEM_LIMIT, collective_id=number, has_side_effects=True
        ),
    )


def dma(*dims):
    return pltpu.SemaphoreType.DMA(dims)


def on_device(
    packets, packet_flow, packet_pos, flow_holder_rank, flow_first_block,
    w_qkv, w_out, w_up, w_down, gain_first, gain_second, head_slopes,
):
    owners, parts = lax.axis_size("flow"), lax.axis_size("tp")
    side = int(round((owners // 2) ** 0.5))
    here, width = packets.shape
    total = owners * KEEP
    chunks = total // TALL
    given = (packets, packet_flow, packet_pos, flow_holder_rank, flow_first_block, gain_first, gain_second)
    box, turned = (side, side, 2, 16, 128), (2, 2, side // 2, side, 16, 128)

    def hold(*dims):
        return pltpu.VMEM(dims, BF16)

    some = hold(chunks, 2, TALL // 2, width)
    full = hold(parts, total, width)
    back, rows = linked(
        functools.partial(layer_kernel, side),
        (shape(*box), shape(here, 128, dtype=F32)),
        [SMEM] + [HBM] * 11,
        [
            *(pltpu.VMEM(v.shape, v.dtype) for v in (*given, w_qkv, w_up, w_down)), hold(parts, *w_out.shape),
            hold(*box), hold(*box), hold(*turned), hold(*turned), hold(*box),
            hold(parts, HEAD_ROWS + total, width), hold(3, total, width), pltpu.VMEM((TALL, total), F32),
            full, full, full, hold(total, width), some, some, some,
            dma(11), dma(2, side), dma(2, side), dma(2, side // 2, 2), dma(2, side // 2, 2),
            dma(side, 2), dma(side, 2), dma(side), dma(side), dma(6), dma(6), dma(2, 6), dma(2, 6),
            dma(chunks, 6), dma(chunks, 6), dma(chunks, 6), dma(chunks, 6),
        ],
        1,
    )(head_slopes, *given, w_qkv, w_out, w_up, w_down)

    return local(final_kernel, (shape(here, width), shape(here, width)), [VMEM] * 2)(
        back.reshape(owners, 16, 128), rows
    )


def solution(mesh):
    return jax.shard_map(
        on_device,
        mesh=mesh,
        in_specs=(
            P("flow", "tp"),
            P("flow"),
            P("flow"),
            P(),
            P(),
            P(None, None, "tp"),
            P("tp", None),
            P(None, "tp"),
            P("tp", None),
            P("tp"),
            P("tp"),
            P("tp"),
        ),
        out_specs=(P("flow", "tp"), P("flow", "tp")),
        check_vma=False,
    )
```

```python
import functools

import jax
import jax.numpy as jnp
from jax import lax
from jax.experimental import pallas as pl
from jax.experimental.pallas import tpu as pltpu
from jax.sharding import PartitionSpec as P

MESH = pl.DeviceIdType.MESH
F32, BF16 = jnp.float32, jnp.bfloat16
D = 1024
BLOCK = 128
KEEP = 5
HEAD_ROWS = 16
HEAD_DIM = 64
EPS = 1e-05
DIGIT = 128
LOG2E = 1.4426950408889634
FAR = 1e30
TALL = 160
VMEM_LIMIT = 56 * 1024 * 1024
VMEM = pl.BlockSpec(memory_space=pltpu.VMEM)
SMEM = pl.BlockSpec(memory_space=pltpu.SMEM)
HBM = pl.BlockSpec(memory_space=pltpu.HBM)


def iota(shape, dim):
    return lax.broadcasted_iota(jnp.int32, shape, dim)


def to_row(column):
    n = column.shape[0]
    eye = iota((n, n), 0) == iota((n, n), 1)
    return jnp.sum(jnp.where(eye, column, 0.0), axis=0, keepdims=True)


def to_column(row):
    n = row.shape[1]
    eye = iota((n, n), 0) == iota((n, n), 1)
    return jnp.sum(jnp.where(eye, row, 0.0), axis=1, keepdims=True)


def onehot(mask):
    return jnp.where(mask, 1.0, 0.0).astype(BF16)


def to_blocks(left, right):
    n = left.shape[0] // 8
    return jnp.concatenate([left.reshape(n, 8, 128), right.reshape(n, 8, 128)], axis=1).astype(BF16)


def from_blocks(blocks):
    n = blocks.shape[0]
    wide = blocks.astype(F32)
    return wide[:, :8].reshape(n * 8, 128).astype(BF16), wide[:, 8:].reshape(n * 8, 128).astype(BF16)


def norm_parts(parts, gains):
    total = sum(jnp.sum(p, axis=1, keepdims=True) for p in parts)
    square = sum(jnp.sum(p * p, axis=1, keepdims=True) for p in parts)
    mean = total / D
    scale = lax.rsqrt(square / D - mean * mean + EPS)
    return [((p - mean) * scale * g).astype(BF16) for p, g in zip(parts, gains)]


def final_kernel(in_ref, pool_ref, rows_ref, enc_ref, ctx_ref):
    left, right = from_blocks(in_ref[...])
    here, rows = rows_ref.shape[0], left.shape[0]
    pick = onehot(iota((here, rows), 1).astype(F32) == rows_ref[:, 0:1])
    enc_ref[:, :128] = jnp.dot(pick, left, preferred_element_type=F32).astype(BF16)
    enc_ref[:, 128:] = jnp.dot(pick, right, preferred_element_type=F32).astype(BF16)
    pool = pool_ref[...]
    at = iota((here, pool.shape[0]), 1).astype(F32)
    for half in range(2):
        pick = onehot(at == rows_ref[:, 1:2] + float(half))
        cols = slice(half * 128, (half + 1) * 128)
        ctx_ref[:, cols] = jnp.dot(pick, pool, preferred_element_type=F32).astype(BF16)


class Spot:
    def __init__(self, side):
        self.side = side
        flow = lax.axis_index("flow")
        self.tp = lax.axis_index("tp")
        self.core = lax.rem(flow, 2)
        chip = lax.div(flow, 2)
        self.y = lax.div(chip, side)
        self.z = lax.rem(chip, side)

    def seen(self, core):
        first = core == 0
        return jnp.where(first, self.y, self.z), jnp.where(first, self.z, self.y)

    def device(self, core, a, b, target_core):
        first = core == 0
        a, b = lax.rem(a + self.side, self.side), lax.rem(b + self.side, self.side)
        y, z = jnp.where(first, a, b), jnp.where(first, b, a)
        return ((y * self.side + z) * 2 + target_core, self.tp)

    def beside(self, step):
        parts = lax.axis_size("tp")
        return (lax.axis_index("flow"), lax.rem(self.tp + step + parts, parts))


def remote(src, dst, send, recv, device):
    return pltpu.make_async_remote_copy(
        src_ref=src, dst_ref=dst, send_sem=send, recv_sem=recv, device_id=device, device_id_type=MESH
    )


def started(copy):
    copy.start()
    return copy


class Ring:
    def __init__(self, spot, src, out, send, recv, cut, start=0, rows=None):
        self.me = spot.tp
        self.right, self.left = spot.beside(1), spot.beside(-1)
        self.src, self.out, self.send, self.recv = src, out, send, recv
        rows = src.shape[0] if rows is None else rows
        self.upper, self.lower = pl.ds(start, cut), pl.ds(start + cut, rows - cut)
        parts = lax.axis_size("tp")
        self.before = lax.rem(self.me + parts - 1, parts)
        self.after = lax.rem(self.me + 1, parts)
        self.far = lax.rem(self.me + 2, parts)

    def copy(self, i, block, part, device, own=False):
        src = self.src.at[part] if own and self.src is not None else self.out.at[block, part]
        return remote(src, self.out.at[block, part], self.send.at[i], self.recv.at[i], device)

    def start(self):
        self.first = [
            self.copy(0, self.me, self.upper, self.right, True),
            self.copy(1, self.me, self.lower, self.left, True),
            self.copy(2, self.me, self.lower, self.right, True),
            self.copy(3, self.me, self.upper, self.left, True),
        ]
        for copy in self.first:
            copy.start()

    def forward(self):
        self.copy(0, self.before, self.upper, self.right).wait_recv()
        self.up = self.copy(4, self.before, self.upper, self.right)
        self.up.start()
        self.copy(1, self.after, self.lower, self.left).wait_recv()
        self.down = self.copy(5, self.after, self.lower, self.left)
        self.down.start()

    def finish(self):
        self.copy(2, self.before, self.lower, self.right).wait_recv()
        self.copy(3, self.after, self.upper, self.left).wait_recv()
        self.copy(4, self.far, self.upper, self.right).wait_recv()
        self.copy(5, self.far, self.lower, self.left).wait_recv()
        for copy in (*self.first, self.up, self.down):
            copy.wait_send()


class Sum:
    def __init__(self, spot, terms, relay, pair, one, send, recv, start, rows):
        parts = lax.axis_size("tp")
        self.me = spot.tp
        self.right, self.left = spot.beside(1), spot.beside(-1)
        self.after, self.before, self.far = (lax.rem(self.me + i, parts) for i in (1, parts - 1, 2))
        self.terms, self.relay, self.pair, self.one = terms, relay, pair, one
        self.send, self.recv = send, recv
        self.upper, self.lower = pl.ds(start, rows // 2), pl.ds(start + rows // 2, rows // 2)

    def copy(self, i, src, dst, device):
        copy = remote(src, dst, self.send.at[i], self.recv.at[i], device)
        copy.start()
        return copy

    def start(self):
        terms = self.terms
        self.copies = [
            self.copy(0, terms.at[self.far, self.upper], self.relay.at[0], self.right),
            self.copy(1, terms.at[self.far, self.lower], self.relay.at[1], self.left),
            self.copy(2, terms.at[self.after, self.lower], self.one.at[1], self.right),
            self.copy(3, terms.at[self.before, self.upper], self.one.at[0], self.left),
        ]

    def forward(self):
        for i, (to, rows, device) in enumerate(
            ((self.after, self.upper, self.right), (self.before, self.lower, self.left))
        ):
            self.copies[i].wait_recv()
            self.relay[i] = (self.relay[i].astype(F32) + self.terms[to, rows, :].astype(F32)).astype(BF16)
            self.copies.append(self.copy(4 + i, self.relay.at[i], self.pair.at[i], device))

    def finish(self, keep, out):
        for i in range(2, 6):
            self.copies[i].wait_recv()
        for i, rows in ((0, self.upper), (1, self.lower)):
            terms = self.terms[self.me, rows, :].astype(F32) + self.pair[i].astype(F32) + self.one[i].astype(F32)
            out[rows, :] = (keep[self.me, rows, :].astype(F32) + terms).astype(BF16)
        for copy in self.copies:
            copy.wait_send()


def pack(spot, packets, flow_row, pos_row, holder, first_block):
    side = spot.side
    a, b = spot.seen(spot.core)
    here, flows = packets.shape[0], holder.shape[1]
    rows = 2 * side * side * 8
    flow = to_column(flow_row)
    pos = to_column(pos_row)
    pick = flow == iota((here, flows), 1).astype(F32)
    dest = jnp.sum(jnp.where(pick, holder, 0.0), axis=1, keepdims=True)
    first = jnp.sum(jnp.where(pick, first_block, 0.0), axis=1, keepdims=True)
    code = first * BLOCK + pos + 1.0
    high = jnp.floor(code * (1.0 / DIGIT))
    low = code - high * DIGIT
    before = (dest == to_row(dest)) & (iota((here, here), 0) > iota((here, here), 1))
    rank = jnp.sum(jnp.where(before, 1.0, 0.0), axis=1, keepdims=True)
    chip = jnp.floor(dest * 0.5)
    half = dest - 2.0 * chip
    major = jnp.floor((chip + 0.5) * (1.0 / side))
    minor = chip - major * side
    swap = spot.core == 1

    def ahead(value, mine):
        value = value - mine.astype(F32)
        return jnp.where(value < 0.0, value + side, value)

    a_off = ahead(jnp.where(swap, minor, major), a)
    b_off = ahead(jnp.where(swap, major, minor), b)
    c_off = jnp.abs(half - spot.core.astype(F32))
    base = ((a_off * side + b_off) * 2.0 + c_off) * 8.0
    odd = b_off - 2.0 * jnp.floor(b_off * 0.5)
    spread = (odd * side + a_off) * 8.0 + rank
    base_row, rank_row = to_row(base), to_row(rank)
    sub = iota((rows, here), 0).astype(F32)
    take = onehot(sub == base_row + rank_row)
    take_high = onehot(sub == base_row + 5.0)
    take_low = onehot(sub == base_row + 6.0)
    mine = iota((here, 128), 1).astype(F32) == spread
    left = (
        jnp.dot(take, packets[:, :128], preferred_element_type=F32)
        + jnp.dot(take_high, jnp.where(mine, high, 0.0).astype(BF16), preferred_element_type=F32)
        + jnp.dot(take_low, jnp.where(mine, low, 0.0).astype(BF16), preferred_element_type=F32)
    )
    right = jnp.dot(take, packets[:, 128:], preferred_element_type=F32)
    at = iota((here, 128), 1)
    pool = base * 0.5 + jnp.where(first > 0.0, 2.0, 0.0)
    return to_blocks(left, right), jnp.where(at == 0, base + rank, pool)


def squeeze(rows, padded, turned=False):
    dims = (padded, rows) if turned else (rows, padded)
    row = iota(dims, 1 if turned else 0).astype(F32)
    place = row + (8 - KEEP) * jnp.floor((row + 0.5) * (1.0 / KEEP))
    return onehot(iota(dims, 0 if turned else 1).astype(F32) == place)


def digits(left):
    rows = left.shape[0]
    groups = rows // 128
    r, g = iota((8, rows), 1), iota((8, rows), 0)
    out = []
    for row in (5, 6):
        pick = onehot((r >= g * 128) & (r < g * 128 + 128) & ((r & 7) == row))
        found = jnp.dot(pick, left, preferred_element_type=F32)
        out.append(jnp.concatenate([found[i : i + 1] for i in range(groups)], axis=1))
    return out


def layer_kernel(
    side, slope_ref, pk_any, flow_any, pos_any, holder_any, first_any, gain1_any, gain2_any,
    wq_any, wo_any, up_any, down_any, back_ref, pool_ref, rows_ref,
    pk_ref, flow_ref, pos_ref, holder_ref, first_ref, gain1_ref, gain2_ref, wq_ref, up_ref, down_ref, wo_ref,
    out_box, mid_ref, in_box, rep_ref, mid2_ref, pool_out, pool_mid, pool_pack,
    all_ref, qkv_ref, far_ref, att_ref, keep_ref, terms_ref, enc_ref, relay, pair, one,
    lsem, s1, r1, s2, r2, s3, r3, s4, r4, s5, r5, s6, r6, wsend, wrecv, asend, arecv, gsend, grecv, ssend, srecv,
):
    spot = Spot(side)
    core, me = spot.core, spot.tp
    other = 1 - core
    a, b = spot.seen(core)
    oa, ob = spot.seen(other)
    rounds, few = 2, side // 2

    barrier = pltpu.get_barrier_semaphore()
    friends = [spot.beside(1), spot.beside(-1), spot.device(core, a, b, other)]
    for i in range(1, side):
        friends += [
            spot.device(core, a + i, b, core), spot.device(core, a, b + i, core),
            spot.device(core, a, b + i, other), spot.device(other, oa, ob + i, other),
        ]
    for device in friends:
        pl.semaphore_signal(barrier, inc=1, device_id=device, device_id_type=MESH)

    sources = (pk_any, flow_any, pos_any, holder_any, first_any, gain1_any, gain2_any, wq_any, up_any, down_any)
    holds = (pk_ref, flow_ref, pos_ref, holder_ref, first_ref, gain1_ref, gain2_ref, wq_ref, up_ref, down_ref)
    loads = [pltpu.make_async_copy(x, h, lsem.at[i]) for i, (x, h) in enumerate(zip(sources, holds))]
    loads.append(pltpu.make_async_copy(wo_any, wo_ref.at[me], lsem.at[len(loads)]))
    for load in loads:
        load.start()
    for load in loads[:7]:
        load.wait()
    flow_row, pos_row, holder, first_block = (
        ref[...].astype(F32)[None] for ref in (flow_ref, pos_ref, holder_ref, first_ref)
    )
    mine = holder == lax.axis_index("flow").astype(F32)
    edge = jnp.max(jnp.where(mine, first_block, 0.0), axis=1, keepdims=True) * BLOCK
    blocks, found = pack(spot, pk_ref[...], flow_row, pos_row, holder, first_block)
    out_box[...] = blocks.reshape(out_box.shape)
    rows_ref[...] = found
    parts, width = all_ref.shape[0], all_ref.shape[2]
    gain_rows = jnp.where(
        iota((HEAD_ROWS, width), 0) == 0, gain1_ref[...].astype(F32)[None], gain2_ref[...].astype(F32)[None]
    ).astype(BF16)
    all_ref[me, :HEAD_ROWS, :] = gain_rows
    pl.semaphore_wait(barrier, len(friends))

    def hop1(h):
        some = pl.ds(h * few, few)
        return [
            started(
                remote(out_box.at[i, some], mid_ref.at[i, some], s1.at[h, i], r1.at[h, i],
                       spot.device(core, a + i, b, core))
            )
            for i in range(1, side)
        ]

    def hop2(h):
        return [
            started(
                remote(mid_ref.at[:, h * few + i, t], in_box.at[h, t, i], s2.at[h, i, t], r2.at[h, i, t],
                       spot.device(core, a, b + h * few + i, core if t == 0 else other))
            )
            for i in range(few) for t in range(2) if h or i or t
        ]

    first = [hop1(0)]
    weights = Ring(spot, wo_any, wo_ref, wsend, wrecv, wo_any.shape[0] // 2)
    weights.start()
    mid_ref[0] = out_box[0]
    for copy in first[0]:
        copy.wait_recv()
    second = [hop2(0)]
    first.append(hop1(1))
    in_box[0, 0, 0] = mid_ref[:, 0, 0]
    for copy in first[1]:
        copy.wait_recv()
    second.append(hop2(1))
    weights.forward()

    sources_here = side * side
    rows = sources_here * KEEP
    total = rounds * rows
    rings, high, low = [], [], []
    for h in range(rounds):
        for copy in second[h]:
            copy.wait_recv()
        left, right = from_blocks(in_box[h].reshape(sources_here, 16, 128))
        keep = squeeze(rows, sources_here * 8)
        here = pl.ds(HEAD_ROWS + h * rows, rows)
        all_ref[me, here, :128] = jnp.dot(keep, left, preferred_element_type=F32).astype(BF16)
        all_ref[me, here, 128:] = jnp.dot(keep, right, preferred_element_type=F32).astype(BF16)
        begin = HEAD_ROWS * (h > 0) + h * rows
        rings.append(
            Ring(spot, None, all_ref, asend.at[h], arecv.at[h], rows // 2, begin, rows + HEAD_ROWS * (h == 0))
        )
        rings[h].start()
        found = digits(left)
        high.append(found[0])
        low.append(found[1])
    both = jnp.where(
        iota((8, total // KEEP * 8), 0) == 0, jnp.concatenate(high, axis=1), jnp.concatenate(low, axis=1)
    ).astype(BF16)
    keep = squeeze(total, total // KEEP * 8)
    across = (((1,), (1,)), ((), ()))
    by_row = lax.dot_general(both, keep, across, preferred_element_type=F32)
    by_column = lax.dot_general(keep, both, across, preferred_element_type=F32)
    slot_row = by_row[0:1] * DIGIT + by_row[1:2] - 1.0
    slot_column = by_column[:, 0:1] * DIGIT + by_column[:, 1:2] - 1.0
    tag_row = jnp.where(slot_row >= edge, 1.0, 0.0)
    tag_column = jnp.where(slot_column >= edge, 1.0, 0.0)

    rings[0].forward()
    loads[7].wait()
    gains = None
    for h in range(rounds):
        if h + 1 < rounds:
            rings[h + 1].forward()
        rings[h].finish()
        if gains is None:
            gains = [all_ref[p, :HEAD_ROWS, :].astype(F32) for p in range(parts)]
        here = pl.ds(HEAD_ROWS + h * rows, rows)
        normed = jnp.concatenate(
            norm_parts([all_ref[p, here, :].astype(F32) for p in range(parts)], [g[0:1] for g in gains]), axis=1
        )
        for k in range(3):
            qkv_ref[k, pl.ds(h * rows, rows), :] = jnp.dot(normed, wq_ref[k], preferred_element_type=F32).astype(BF16)

    def attend(chunk):
        rows = pl.ds(chunk * TALL, TALL)
        part = slice(chunk * TALL, (chunk + 1) * TALL)
        itself = iota((TALL, total), 0) + chunk * TALL == iota((TALL, total), 1)
        allowed = ((tag_column[part] == tag_row) & (slot_row >= 0.0)) | itself
        far_ref[...] = jnp.where(allowed, jnp.abs(slot_column[part] - slot_row) * LOG2E, FAR)
        first = iota((TALL, 128), 1) < HEAD_DIM
        for two in range(width // 128):
            cols = slice(two * 128, (two + 1) * 128)
            query = qkv_ref[0, rows, cols]
            keys, values = qkv_ref[1, :, cols], qkv_ref[2, :, cols]
            halves = []
            for half in range(2):
                mine = jnp.where(first == (half == 0), query, jnp.zeros_like(query))
                scores = lax.dot_general(mine, keys, across, preferred_element_type=F32)
                weights = jnp.exp2(
                    scores * (HEAD_DIM**-0.5 * LOG2E) - slope_ref[2 * two + half] * far_ref[...]
                )
                probs = weights * (1.0 / jnp.sum(weights, axis=1, keepdims=True))
                halves.append(jnp.dot(probs.astype(BF16), values, preferred_element_type=F32))
            att_ref[me, rows, cols] = jnp.where(first, halves[0], halves[1]).astype(BF16)

    def forward_layer(chunk):
        rows = pl.ds(chunk * TALL, TALL)
        there = pl.ds(HEAD_ROWS + chunk * TALL, TALL)
        attn = sum(
            jnp.dot(att_ref[p, rows, :], wo_ref[p], preferred_element_type=F32).astype(BF16).astype(F32)
            for p in range(parts)
        )
        middle = [
            (all_ref[p, there, :].astype(F32) + attn[:, p * width : (p + 1) * width]).astype(BF16)
            for p in range(parts)
        ]
        for p in range(parts):
            keep_ref[p, rows, :] = middle[p]
        normed = jnp.concatenate(norm_parts([m.astype(F32) for m in middle], [g[1:2] for g in gains]), axis=1)
        upward = jnp.dot(normed, up_ref[...], preferred_element_type=F32)
        active = (0.5 * upward * (1.0 + lax.erf(upward * (0.5**0.5)))).astype(BF16)
        for p in range(parts):
            terms_ref[p, rows, :] = jnp.dot(
                active, down_ref[:, p * width : (p + 1) * width], preferred_element_type=F32
            ).astype(BF16)

    chunks = total // TALL
    rings = [Ring(spot, None, att_ref, gsend.at[c], grecv.at[c], TALL // 2, c * TALL, TALL) for c in range(chunks)]
    sums = [
        Sum(spot, terms_ref, relay.at[c], pair.at[c], one.at[c], ssend.at[c], srecv.at[c], c * TALL, TALL)
        for c in range(chunks)
    ]
    for c in range(chunks):
        attend(c)
        rings[c].start()
        if c:
            rings[c - 1].forward()
    third, fourth, moved = [[] for _ in range(rounds)], [], []

    def toward(far, t):
        frame, fa, fb = (core, a, b) if t == 0 else (other, oa, ob)
        return spot.device(frame, fa, fb - far, frame)

    def reply(c):
        sums[c].finish(keep_ref, enc_ref)
        h, t = c // 2, c % 2
        spread = squeeze(TALL, TALL // KEEP * 8, True)
        wide = jnp.dot(spread, enc_ref[pl.ds(c * TALL, TALL), :], preferred_element_type=F32)
        rep_ref[h, t] = to_blocks(wide[:, :128], wide[:, 128:]).reshape(few, side, 16, 128)
        for i in range(few):
            far = h * few + i
            if far or t:
                third[h].append(
                    started(
                        remote(rep_ref.at[h, t, i], mid2_ref.at[:, far, t], s3.at[far, t], r3.at[far, t],
                               toward(far, t))
                    )
                )
            else:
                mid2_ref[:, 0, 0] = rep_ref[0, 0, 0]

    def relay_back(h):
        for copy in third[h]:
            copy.wait_recv()
        some = pl.ds(h * few, few)
        for i in range(1, side):
            fourth.append(
                started(
                    remote(mid2_ref.at[i, some], back_ref.at[i, some], s4.at[h, i], r4.at[h, i],
                           spot.device(core, a - i, b, core))
                )
            )
        back_ref[0, some] = mid2_ref[0, some]

    weights.finish()
    for load in loads[8:]:
        load.wait()
    for c in range(chunks):
        if c == 1:
            rings[chunks - 1].forward()
        rings[c].finish()
        forward_layer(c)
        sums[c].start()
        if c:
            sums[c - 1].forward()
    reply(0)
    reply(1)
    sums[3].forward()
    reply(2)
    relay_back(0)
    reply(3)

    encoded = enc_ref[...]
    number = iota((8, total), 0).astype(F32)
    members = jnp.where((slot_row >= 0.0) & (tag_row == number), 1.0, 0.0)
    counts = jnp.sum(members, axis=1, keepdims=True)
    pooled = jnp.dot(members.astype(BF16), encoded, preferred_element_type=F32) / counts
    lane = iota((16, 128), 0)
    four = [
        jnp.where((lane & 2) == 0, pooled[0:1, cols], pooled[1:2, cols]) for cols in (slice(0, 128), slice(128, 256))
    ]
    pool_out[...] = jnp.where((lane & 1) == 0, four[0], four[1]).astype(BF16)
    for far in range(side):
        for t in range(2):
            if far or t:
                moved.append(
                    started(remote(pool_out, pool_mid.at[far, t], s5.at[far, t], r5.at[far, t], toward(far, t)))
                )
    pool_mid[0, 0] = pool_out[...]
    relay_back(1)
    for copy in moved:
        copy.wait_recv()
    quarter = lax.shift_right_logical(iota((side // 2, 16, 128), 1), 2)
    grouped = pool_mid[...].astype(F32).reshape(side // 2, 4, 16, 128)
    packed = grouped[:, 0]
    for i in range(1, 4):
        packed = jnp.where(quarter == i, grouped[:, i], packed)
    pool_pack[...] = packed.astype(BF16)
    last = [
        started(remote(pool_pack, pool_ref.at[i], s6.at[i], r6.at[i], spot.device(core, a - i, b, core)))
        for i in range(1, side)
    ]
    pool_ref[0] = pool_pack[...]
    for copy in (*fourth, *last):
        copy.wait_recv()
    for copy in (*first[0], *first[1], *second[0], *second[1], *third[0], *third[1], *fourth, *moved, *last):
        copy.wait_send()


def shape(*dims, dtype=BF16):
    return jax.ShapeDtypeStruct(dims, dtype)


def local(kernel, outs, specs, scratch=()):
    return pl.pallas_call(
        kernel,
        out_shape=outs,
        in_specs=specs,
        out_specs=jax.tree.map(lambda _: VMEM, outs),
        scratch_shapes=list(scratch),
        compiler_params=pltpu.CompilerParams(vmem_limit_bytes=VMEM_LIMIT),
    )


def linked(kernel, outs, inputs, scratch, number):
    return pl.pallas_call(
        kernel,
        out_shape=outs,
        in_specs=[VMEM] * inputs if isinstance(inputs, int) else inputs,
        out_specs=jax.tree.map(lambda _: VMEM, outs),
        scratch_shapes=scratch,
        compiler_params=pltpu.CompilerParams(
            vmem_limit_bytes=VMEM_LIMIT, collective_id=number, has_side_effects=True
        ),
    )


def dma(*dims):
    return pltpu.SemaphoreType.DMA(dims)


def on_device(
    packets, packet_flow, packet_pos, flow_holder_rank, flow_first_block,
    w_qkv, w_out, w_up, w_down, gain_first, gain_second, head_slopes,
):
    owners, parts = lax.axis_size("flow"), lax.axis_size("tp")
    side = int(round((owners // 2) ** 0.5))
    here, width = packets.shape
    total = owners * KEEP
    chunks = total // TALL
    given = (packets, packet_flow, packet_pos, flow_holder_rank, flow_first_block, gain_first, gain_second)
    box, turned = (side, side, 2, 16, 128), (2, 2, side // 2, side, 16, 128)

    def hold(*dims):
        return pltpu.VMEM(dims, BF16)

    some = hold(chunks, 2, TALL // 2, width)
    full = hold(parts, total, width)
    back, pool, rows = linked(
        functools.partial(layer_kernel, side),
        (shape(*box), shape(side, side // 2, 16, 128), shape(here, 128, dtype=F32)),
        [SMEM] + [HBM] * 11,
        [
            *(pltpu.VMEM(v.shape, v.dtype) for v in (*given, w_qkv, w_up, w_down)), hold(parts, *w_out.shape),
            hold(*box), hold(*box), hold(*turned), hold(*turned), hold(*box),
            hold(16, 128), hold(side, 2, 16, 128), hold(side // 2, 16, 128),
            hold(parts, HEAD_ROWS + total, width), hold(3, total, width), pltpu.VMEM((TALL, total), F32),
            full, full, full, hold(total, width), some, some, some,
            dma(11), dma(2, side), dma(2, side), dma(2, side // 2, 2), dma(2, side // 2, 2),
            dma(side, 2), dma(side, 2), dma(2, side), dma(2, side), dma(side, 2), dma(side, 2), dma(side), dma(side), dma(6), dma(6), dma(2, 6), dma(2, 6),
            dma(chunks, 6), dma(chunks, 6), dma(chunks, 6), dma(chunks, 6),
        ],
        1,
    )(head_slopes, *given, w_qkv, w_out, w_up, w_down)

    return local(final_kernel, (shape(here, width), shape(here, width)), [VMEM] * 3)(
        back.reshape(owners, 16, 128), pool.reshape(owners * 4, 128), rows
    )


def solution(mesh):
    return jax.shard_map(
        on_device,
        mesh=mesh,
        in_specs=(
            P("flow", "tp"),
            P("flow"),
            P("flow"),
            P(),
            P(),
            P(None, None, "tp"),
            P("tp", None),
            P(None, "tp"),
            P("tp", None),
            P("tp"),
            P("tp"),
            P("tp"),
        ),
        out_specs=(P("flow", "tp"), P("flow", "tp")),
        check_vma=False,
    )
```

```python
import functools

import jax
import jax.numpy as jnp
from jax import lax
from jax.experimental import pallas as pl
from jax.experimental.pallas import tpu as pltpu
from jax.sharding import PartitionSpec as P

MESH = pl.DeviceIdType.MESH
F32, BF16 = jnp.float32, jnp.bfloat16
D = 1024
BLOCK = 128
KEEP = 5
HEAD_ROWS = 16
HEAD_DIM = 64
EPS = 1e-05
DIGIT = 128
LOG2E = 1.4426950408889634
FAR = 1e30
TALL = 160
VMEM_LIMIT = 56 * 1024 * 1024
VMEM = pl.BlockSpec(memory_space=pltpu.VMEM)
SMEM = pl.BlockSpec(memory_space=pltpu.SMEM)
HBM = pl.BlockSpec(memory_space=pltpu.HBM)


def iota(shape, dim):
    return lax.broadcasted_iota(jnp.int32, shape, dim)


def to_row(column):
    n = column.shape[0]
    eye = iota((n, n), 0) == iota((n, n), 1)
    return jnp.sum(jnp.where(eye, column, 0.0), axis=0, keepdims=True)


def to_column(row):
    n = row.shape[1]
    eye = iota((n, n), 0) == iota((n, n), 1)
    return jnp.sum(jnp.where(eye, row, 0.0), axis=1, keepdims=True)


def onehot(mask):
    return jnp.where(mask, 1.0, 0.0).astype(BF16)


def to_blocks(left, right):
    n = left.shape[0] // 8
    return jnp.concatenate([left.reshape(n, 8, 128), right.reshape(n, 8, 128)], axis=1).astype(BF16)


def from_blocks(blocks):
    n = blocks.shape[0]
    wide = blocks.astype(F32)
    return wide[:, :8].reshape(n * 8, 128).astype(BF16), wide[:, 8:].reshape(n * 8, 128).astype(BF16)


def norm_parts(parts, gains):
    total = sum(jnp.sum(p, axis=1, keepdims=True) for p in parts)
    square = sum(jnp.sum(p * p, axis=1, keepdims=True) for p in parts)
    mean = total / D
    scale = lax.rsqrt(square / D - mean * mean + EPS)
    return [((p - mean) * scale * g).astype(BF16) for p, g in zip(parts, gains)]


def final_kernel(in_ref, rows_ref, enc_ref, ctx_ref):
    given = jnp.concatenate(from_blocks(in_ref[...]), axis=1)
    at = iota((rows_ref.shape[0], given.shape[0]), 1).astype(F32)
    for column, out in ((0, enc_ref), (1, ctx_ref)):
        pick = onehot(at == rows_ref[:, column : column + 1])
        out[...] = jnp.dot(pick, given, preferred_element_type=F32).astype(BF16)


class Spot:
    def __init__(self, side):
        self.side = side
        flow = lax.axis_index("flow")
        self.tp = lax.axis_index("tp")
        self.core = lax.rem(flow, 2)
        chip = lax.div(flow, 2)
        self.y = lax.div(chip, side)
        self.z = lax.rem(chip, side)

    def seen(self, core):
        first = core == 0
        return jnp.where(first, self.y, self.z), jnp.where(first, self.z, self.y)

    def device(self, core, a, b, target_core):
        first = core == 0
        a, b = lax.rem(a + self.side, self.side), lax.rem(b + self.side, self.side)
        y, z = jnp.where(first, a, b), jnp.where(first, b, a)
        return ((y * self.side + z) * 2 + target_core, self.tp)

    def beside(self, step):
        parts = lax.axis_size("tp")
        return (lax.axis_index("flow"), lax.rem(self.tp + step + parts, parts))


def remote(src, dst, send, recv, device):
    return pltpu.make_async_remote_copy(
        src_ref=src, dst_ref=dst, send_sem=send, recv_sem=recv, device_id=device, device_id_type=MESH
    )


def started(copy):
    copy.start()
    return copy


class Ring:
    def __init__(self, spot, src, out, send, recv, cut, start=0, rows=None):
        self.me = spot.tp
        self.right, self.left = spot.beside(1), spot.beside(-1)
        self.src, self.out, self.send, self.recv = src, out, send, recv
        rows = src.shape[0] if rows is None else rows
        self.upper, self.lower = pl.ds(start, cut), pl.ds(start + cut, rows - cut)
        parts = lax.axis_size("tp")
        self.before = lax.rem(self.me + parts - 1, parts)
        self.after = lax.rem(self.me + 1, parts)
        self.far = lax.rem(self.me + 2, parts)

    def copy(self, i, block, part, device, own=False):
        src = self.src.at[part] if own and self.src is not None else self.out.at[block, part]
        return remote(src, self.out.at[block, part], self.send.at[i], self.recv.at[i], device)

    def start(self):
        self.first = [
            self.copy(0, self.me, self.upper, self.right, True),
            self.copy(1, self.me, self.lower, self.left, True),
            self.copy(2, self.me, self.lower, self.right, True),
            self.copy(3, self.me, self.upper, self.left, True),
        ]
        for copy in self.first:
            copy.start()

    def forward(self):
        self.copy(0, self.before, self.upper, self.right).wait_recv()
        self.up = self.copy(4, self.before, self.upper, self.right)
        self.up.start()
        self.copy(1, self.after, self.lower, self.left).wait_recv()
        self.down = self.copy(5, self.after, self.lower, self.left)
        self.down.start()

    def finish(self):
        self.copy(2, self.before, self.lower, self.right).wait_recv()
        self.copy(3, self.after, self.upper, self.left).wait_recv()
        self.copy(4, self.far, self.upper, self.right).wait_recv()
        self.copy(5, self.far, self.lower, self.left).wait_recv()
        for copy in (*self.first, self.up, self.down):
            copy.wait_send()


class Sum:
    def __init__(self, spot, terms, relay, pair, one, send, recv, start, rows):
        parts = lax.axis_size("tp")
        self.me = spot.tp
        self.right, self.left = spot.beside(1), spot.beside(-1)
        self.after, self.before, self.far = (lax.rem(self.me + i, parts) for i in (1, parts - 1, 2))
        self.terms, self.relay, self.pair, self.one = terms, relay, pair, one
        self.send, self.recv = send, recv
        self.upper, self.lower = pl.ds(start, rows // 2), pl.ds(start + rows // 2, rows // 2)

    def copy(self, i, src, dst, device):
        copy = remote(src, dst, self.send.at[i], self.recv.at[i], device)
        copy.start()
        return copy

    def start(self):
        terms = self.terms
        self.copies = [
            self.copy(0, terms.at[self.far, self.upper], self.relay.at[0], self.right),
            self.copy(1, terms.at[self.far, self.lower], self.relay.at[1], self.left),
            self.copy(2, terms.at[self.after, self.lower], self.one.at[1], self.right),
            self.copy(3, terms.at[self.before, self.upper], self.one.at[0], self.left),
        ]

    def forward(self):
        for i, (to, rows, device) in enumerate(
            ((self.after, self.upper, self.right), (self.before, self.lower, self.left))
        ):
            self.copies[i].wait_recv()
            self.relay[i] = (self.relay[i].astype(F32) + self.terms[to, rows, :].astype(F32)).astype(BF16)
            self.copies.append(self.copy(4 + i, self.relay.at[i], self.pair.at[i], device))

    def finish(self, keep, out):
        for i in range(2, 6):
            self.copies[i].wait_recv()
        for i, rows in ((0, self.upper), (1, self.lower)):
            terms = self.terms[self.me, rows, :].astype(F32) + self.pair[i].astype(F32) + self.one[i].astype(F32)
            out[rows, :] = (keep[self.me, rows, :].astype(F32) + terms).astype(BF16)
        for copy in self.copies:
            copy.wait_send()


def pack(spot, packets, flow_row, pos_row, holder, first_block):
    side = spot.side
    a, b = spot.seen(spot.core)
    here, flows = packets.shape[0], holder.shape[1]
    rows = 2 * side * side * 8
    flow = to_column(flow_row)
    pos = to_column(pos_row)
    pick = flow == iota((here, flows), 1).astype(F32)
    dest = jnp.sum(jnp.where(pick, holder, 0.0), axis=1, keepdims=True)
    first = jnp.sum(jnp.where(pick, first_block, 0.0), axis=1, keepdims=True)
    code = first * BLOCK + pos + 1.0
    high = jnp.floor(code * (1.0 / DIGIT))
    low = code - high * DIGIT
    before = (dest == to_row(dest)) & (iota((here, here), 0) > iota((here, here), 1))
    rank = jnp.sum(jnp.where(before, 1.0, 0.0), axis=1, keepdims=True)
    chip = jnp.floor(dest * 0.5)
    half = dest - 2.0 * chip
    major = jnp.floor((chip + 0.5) * (1.0 / side))
    minor = chip - major * side
    swap = spot.core == 1

    def ahead(value, mine):
        value = value - mine.astype(F32)
        return jnp.where(value < 0.0, value + side, value)

    a_off = ahead(jnp.where(swap, minor, major), a)
    b_off = ahead(jnp.where(swap, major, minor), b)
    c_off = jnp.abs(half - spot.core.astype(F32))
    base = ((a_off * side + b_off) * 2.0 + c_off) * 8.0
    odd = b_off - 2.0 * jnp.floor(b_off * 0.5)
    spread = (odd * side + a_off) * 8.0 + rank
    base_row, rank_row = to_row(base), to_row(rank)
    sub = iota((rows, here), 0).astype(F32)
    take = onehot(sub == base_row + rank_row)
    take_high = onehot(sub == base_row + 5.0)
    take_low = onehot(sub == base_row + 6.0)
    mine = iota((here, 128), 1).astype(F32) == spread
    left = (
        jnp.dot(take, packets[:, :128], preferred_element_type=F32)
        + jnp.dot(take_high, jnp.where(mine, high, 0.0).astype(BF16), preferred_element_type=F32)
        + jnp.dot(take_low, jnp.where(mine, low, 0.0).astype(BF16), preferred_element_type=F32)
    )
    right = jnp.dot(take, packets[:, 128:], preferred_element_type=F32)
    at = iota((here, 128), 1)
    pool = base + 5.0 + jnp.where(first > 0.0, 1.0, 0.0)
    return to_blocks(left, right), jnp.where(at == 0, base + rank, pool)


def squeeze(rows, padded, turned=False):
    dims = (padded, rows) if turned else (rows, padded)
    row = iota(dims, 1 if turned else 0).astype(F32)
    place = row + (8 - KEEP) * jnp.floor((row + 0.5) * (1.0 / KEEP))
    return onehot(iota(dims, 0 if turned else 1).astype(F32) == place)


def digits(left):
    rows = left.shape[0]
    groups = rows // 128
    r, g = iota((8, rows), 1), iota((8, rows), 0)
    out = []
    for row in (5, 6):
        pick = onehot((r >= g * 128) & (r < g * 128 + 128) & ((r & 7) == row))
        found = jnp.dot(pick, left, preferred_element_type=F32)
        out.append(jnp.concatenate([found[i : i + 1] for i in range(groups)], axis=1))
    return out


def layer_kernel(
    side, slope_ref, pk_any, flow_any, pos_any, holder_any, first_any, gain1_any, gain2_any,
    wq_any, wo_any, up_any, down_any, back_ref, rows_ref,
    pk_ref, flow_ref, pos_ref, holder_ref, first_ref, gain1_ref, gain2_ref, wq_ref, up_ref, down_ref, wo_ref,
    out_box, mid_ref, in_box, rep_ref, mid2_ref,
    all_ref, qkv_ref, far_ref, att_ref, keep_ref, terms_ref, enc_ref, relay, pair, one,
    lsem, s1, r1, s2, r2, s3, r3, s4, r4, wsend, wrecv, asend, arecv, gsend, grecv, ssend, srecv,
):
    spot = Spot(side)
    core, me = spot.core, spot.tp
    other = 1 - core
    a, b = spot.seen(core)
    oa, ob = spot.seen(other)
    rounds, few = 2, side // 2

    barrier = pltpu.get_barrier_semaphore()
    friends = [spot.beside(1), spot.beside(-1), spot.device(core, a, b, other)]
    for i in range(1, side):
        friends += [
            spot.device(core, a + i, b, core), spot.device(core, a, b + i, core),
            spot.device(core, a, b + i, other), spot.device(other, oa, ob + i, other),
        ]
    sources = (pk_any, flow_any, pos_any, holder_any, first_any, gain1_any, gain2_any, wq_any, up_any, down_any)
    holds = (pk_ref, flow_ref, pos_ref, holder_ref, first_ref, gain1_ref, gain2_ref, wq_ref, up_ref, down_ref)
    loads = [pltpu.make_async_copy(x, h, lsem.at[i]) for i, (x, h) in enumerate(zip(sources, holds))]
    share = wo_any.shape[0] // 2
    begin = pl.multiple_of(core * share, share)
    our = pl.ds(begin, share)
    loads.append(pltpu.make_async_copy(wo_any.at[our], wo_ref.at[me, our], lsem.at[len(loads)]))
    for load in loads[:7]:
        load.start()
    for device in friends:
        pl.semaphore_signal(barrier, inc=1, device_id=device, device_id_type=MESH)
    for load in loads[7:]:
        load.start()
    for load in loads[:7]:
        load.wait()
    flow_row, pos_row, holder, first_block = (
        ref[...].astype(F32)[None] for ref in (flow_ref, pos_ref, holder_ref, first_ref)
    )
    mine = holder == lax.axis_index("flow").astype(F32)
    edge = jnp.max(jnp.where(mine, first_block, 0.0), axis=1, keepdims=True) * BLOCK
    blocks, found = pack(spot, pk_ref[...], flow_row, pos_row, holder, first_block)
    out_box[...] = blocks.reshape(out_box.shape)
    rows_ref[...] = found
    parts, width = all_ref.shape[0], all_ref.shape[2]
    gain_rows = jnp.where(
        iota((HEAD_ROWS, width), 0) == 0, gain1_ref[...].astype(F32)[None], gain2_ref[...].astype(F32)[None]
    ).astype(BF16)
    all_ref[me, :HEAD_ROWS, :] = gain_rows
    pl.semaphore_wait(barrier, len(friends))

    def hop1(h):
        some = pl.ds(h * few, few)
        return [
            started(
                remote(out_box.at[i, some], mid_ref.at[i, some], s1.at[h, i], r1.at[h, i],
                       spot.device(core, a + i, b, core))
            )
            for i in range(1, side)
        ]

    def hop2(h):
        return [
            started(
                remote(mid_ref.at[:, h * few + i, t], in_box.at[h, t, i], s2.at[h, i, t], r2.at[h, i, t],
                       spot.device(core, a, b + h * few + i, core if t == 0 else other))
            )
            for i in range(few) for t in range(2) if h or i or t
        ]

    first = [hop1(0), hop1(1)]
    weights = Ring(spot, wo_any, wo_ref, wsend, wrecv, share // 2, begin, share)
    weights.start()
    mid_ref[0] = out_box[0]
    for copy in first[0]:
        copy.wait_recv()
    second = [hop2(0)]
    in_box[0, 0, 0] = mid_ref[:, 0, 0]
    weights.forward()
    for copy in first[1]:
        copy.wait_recv()
    second.append(hop2(1))
    weights.finish()
    loads[10].wait()
    swap = started(
        remote(wo_ref.at[:, our], wo_ref.at[:, our], wsend.at[6], wrecv.at[6], spot.device(core, a, b, other))
    )

    sources_here = side * side
    rows = sources_here * KEEP
    total = rounds * rows
    rings, high, low = [], [], []
    for h in range(rounds):
        for copy in second[h]:
            copy.wait_recv()
        left, right = from_blocks(in_box[h].reshape(sources_here, 16, 128))
        keep = squeeze(rows, sources_here * 8)
        here = pl.ds(HEAD_ROWS + h * rows, rows)
        all_ref[me, here, :128] = jnp.dot(keep, left, preferred_element_type=F32).astype(BF16)
        all_ref[me, here, 128:] = jnp.dot(keep, right, preferred_element_type=F32).astype(BF16)
        begin = HEAD_ROWS * (h > 0) + h * rows
        rings.append(
            Ring(spot, None, all_ref, asend.at[h], arecv.at[h], rows // 2, begin, rows + HEAD_ROWS * (h == 0))
        )
        rings[h].start()
        found = digits(left)
        high.append(found[0])
        low.append(found[1])
    both = jnp.where(
        iota((8, total // KEEP * 8), 0) == 0, jnp.concatenate(high, axis=1), jnp.concatenate(low, axis=1)
    ).astype(BF16)
    keep = squeeze(total, total // KEEP * 8)
    across = (((1,), (1,)), ((), ()))
    by_row = lax.dot_general(both, keep, across, preferred_element_type=F32)
    by_column = lax.dot_general(keep, both, across, preferred_element_type=F32)
    slot_row = by_row[0:1] * DIGIT + by_row[1:2] - 1.0
    slot_column = by_column[:, 0:1] * DIGIT + by_column[:, 1:2] - 1.0
    tag_row = jnp.where(slot_row >= edge, 1.0, 0.0)
    tag_column = jnp.where(slot_column >= edge, 1.0, 0.0)

    rings[0].forward()
    loads[7].wait()
    gains = None
    for h in range(rounds):
        if h + 1 < rounds:
            rings[h + 1].forward()
        rings[h].finish()
        if gains is None:
            gains = [all_ref[p, :HEAD_ROWS, :].astype(F32) for p in range(parts)]
        here = pl.ds(HEAD_ROWS + h * rows, rows)
        normed = jnp.concatenate(
            norm_parts([all_ref[p, here, :].astype(F32) for p in range(parts)], [g[0:1] for g in gains]), axis=1
        )
        for k in range(3):
            qkv_ref[k, pl.ds(h * rows, rows), :] = jnp.dot(normed, wq_ref[k], preferred_element_type=F32).astype(BF16)

    number = iota((8, total), 0).astype(F32)
    members = jnp.where((slot_row >= 0.0) & (tag_row == number), 1.0, 0.0)
    counts = jnp.sum(members, axis=1, keepdims=True)

    def attend(chunk):
        rows = pl.ds(chunk * TALL, TALL)
        part = slice(chunk * TALL, (chunk + 1) * TALL)
        itself = iota((TALL, total), 0) + chunk * TALL == iota((TALL, total), 1)
        allowed = ((tag_column[part] == tag_row) & (slot_row >= 0.0)) | itself
        far_ref[...] = jnp.where(allowed, jnp.abs(slot_column[part] - slot_row) * LOG2E, FAR)
        first = iota((TALL, 128), 1) < HEAD_DIM
        for two in range(width // 128):
            cols = slice(two * 128, (two + 1) * 128)
            query = qkv_ref[0, rows, cols]
            keys, values = qkv_ref[1, :, cols], qkv_ref[2, :, cols]
            halves = []
            for half in range(2):
                mine = jnp.where(first == (half == 0), query, jnp.zeros_like(query))
                scores = lax.dot_general(mine, keys, across, preferred_element_type=F32)
                weights = jnp.exp2(
                    scores * (HEAD_DIM**-0.5 * LOG2E) - slope_ref[2 * two + half] * far_ref[...]
                )
                probs = weights * (1.0 / jnp.sum(weights, axis=1, keepdims=True))
                halves.append(jnp.dot(probs.astype(BF16), values, preferred_element_type=F32))
            att_ref[me, rows, cols] = jnp.where(first, halves[0], halves[1]).astype(BF16)

    def forward_layer(chunk):
        rows = pl.ds(chunk * TALL, TALL)
        there = pl.ds(HEAD_ROWS + chunk * TALL, TALL)
        attn = sum(
            jnp.dot(att_ref[p, rows, :], wo_ref[p], preferred_element_type=F32).astype(BF16).astype(F32)
            for p in range(parts)
        )
        middle = [
            (all_ref[p, there, :].astype(F32) + attn[:, p * width : (p + 1) * width]).astype(BF16)
            for p in range(parts)
        ]
        for p in range(parts):
            keep_ref[p, rows, :] = middle[p]
        normed = jnp.concatenate(norm_parts([m.astype(F32) for m in middle], [g[1:2] for g in gains]), axis=1)
        upward = jnp.dot(normed, up_ref[...], preferred_element_type=F32)
        active = (0.5 * upward * (1.0 + lax.erf(upward * (0.5**0.5)))).astype(BF16)
        for p in range(parts):
            terms_ref[p, rows, :] = jnp.dot(
                active, down_ref[:, p * width : (p + 1) * width], preferred_element_type=F32
            ).astype(BF16)

    chunks = total // TALL
    rings = [Ring(spot, None, att_ref, gsend.at[c], grecv.at[c], TALL // 2, c * TALL, TALL) for c in range(chunks)]
    sums = [
        Sum(spot, terms_ref, relay.at[c], pair.at[c], one.at[c], ssend.at[c], srecv.at[c], c * TALL, TALL)
        for c in range(chunks)
    ]
    for c in range(chunks):
        attend(c)
        rings[c].start()
        if c:
            rings[c - 1].forward()
    theirs = pl.ds(pl.multiple_of(other * share, share), share)
    remote(
        wo_ref.at[:, theirs], wo_ref.at[:, theirs], wsend.at[6], wrecv.at[6], spot.device(core, a, b, other)
    ).wait_recv()
    for load in loads[8:10]:
        load.wait()
    for c in range(chunks):
        if c == 1:
            rings[chunks - 1].forward()
        rings[c].finish()
        forward_layer(c)
        sums[c].start()
        if c:
            sums[c - 1].forward()
    expand = squeeze(TALL, TALL // KEEP * 8, True)

    def settle(c):
        sums[c].finish(keep_ref, enc_ref)
        wide = jnp.dot(expand, enc_ref[pl.ds(c * TALL, TALL), :], preferred_element_type=F32)
        rep_ref[c // 2, c % 2] = to_blocks(wide[:, :128], wide[:, 128:]).reshape(few, side, 16, 128)

    settle(0)
    settle(1)
    sums[chunks - 1].forward()
    settle(2)
    settle(3)

    pooled = jnp.dot(members.astype(BF16), enc_ref[...], preferred_element_type=F32) / counts
    line = iota((16, 128), 0)
    near = jnp.where(line < 8, pooled[0:1, :128], pooled[0:1, 128:])
    next_to = jnp.where(line < 8, pooled[1:2, :128], pooled[1:2, 128:])
    tile = jnp.where((line & 7) == 5, near, jnp.where((line & 7) == 6, next_to, 0.0)).astype(BF16)
    rep_ref[...] = rep_ref[...] + tile

    third, fourth = [[] for _ in range(rounds)], []
    for h in range(rounds):
        for i in range(few):
            for t in range(2):
                if h or i or t:
                    frame, fa, fb = (core, a, b) if t == 0 else (other, oa, ob)
                    far = h * few + i
                    third[h].append(
                        started(
                            remote(rep_ref.at[h, t, i], mid2_ref.at[:, far, t], s3.at[far, t], r3.at[far, t],
                                   spot.device(frame, fa, fb - far, frame))
                        )
                    )
    mid2_ref[:, 0, 0] = rep_ref[0, 0, 0]
    for h in range(rounds):
        for copy in third[h]:
            copy.wait_recv()
        some = pl.ds(h * few, few)
        for i in range(1, side):
            fourth.append(
                started(
                    remote(mid2_ref.at[i, some], back_ref.at[i, some], s4.at[h, i], r4.at[h, i],
                           spot.device(core, a - i, b, core))
                )
            )
        back_ref[0, some] = mid2_ref[0, some]
    for copy in fourth:
        copy.wait_recv()
    for copy in (*first[0], *first[1], *second[0], *second[1], *third[0], *third[1], *fourth, swap):
        copy.wait_send()


def shape(*dims, dtype=BF16):
    return jax.ShapeDtypeStruct(dims, dtype)


def local(kernel, outs, specs, scratch=()):
    return pl.pallas_call(
        kernel,
        out_shape=outs,
        in_specs=specs,
        out_specs=jax.tree.map(lambda _: VMEM, outs),
        scratch_shapes=list(scratch),
        compiler_params=pltpu.CompilerParams(vmem_limit_bytes=VMEM_LIMIT),
    )


def linked(kernel, outs, inputs, scratch, number):
    return pl.pallas_call(
        kernel,
        out_shape=outs,
        in_specs=[VMEM] * inputs if isinstance(inputs, int) else inputs,
        out_specs=jax.tree.map(lambda _: VMEM, outs),
        scratch_shapes=scratch,
        compiler_params=pltpu.CompilerParams(
            vmem_limit_bytes=VMEM_LIMIT, collective_id=number, has_side_effects=True
        ),
    )


def dma(*dims):
    return pltpu.SemaphoreType.DMA(dims)


def on_device(
    packets, packet_flow, packet_pos, flow_holder_rank, flow_first_block,
    w_qkv, w_out, w_up, w_down, gain_first, gain_second, head_slopes,
):
    owners, parts = lax.axis_size("flow"), lax.axis_size("tp")
    side = int(round((owners // 2) ** 0.5))
    here, width = packets.shape
    total = owners * KEEP
    chunks = total // TALL
    given = (packets, packet_flow, packet_pos, flow_holder_rank, flow_first_block, gain_first, gain_second)
    box, turned = (side, side, 2, 16, 128), (2, 2, side // 2, side, 16, 128)

    def hold(*dims):
        return pltpu.VMEM(dims, BF16)

    some = hold(chunks, 2, TALL // 2, width)
    full = hold(parts, total, width)
    back, rows = linked(
        functools.partial(layer_kernel, side),
        (shape(*box), shape(here, 128, dtype=F32)),
        [SMEM] + [HBM] * 11,
        [
            *(pltpu.VMEM(v.shape, v.dtype) for v in (*given, w_qkv, w_up, w_down)), hold(parts, *w_out.shape),
            hold(*box), hold(*box), hold(*turned), hold(*turned), hold(*box),
            hold(parts, HEAD_ROWS + total, width), hold(3, total, width), pltpu.VMEM((TALL, total), F32),
            full, full, full, hold(total, width), some, some, some,
            dma(11), dma(2, side), dma(2, side), dma(2, side // 2, 2), dma(2, side // 2, 2),
            dma(side, 2), dma(side, 2), dma(2, side), dma(2, side), dma(7), dma(7), dma(2, 6), dma(2, 6),
            dma(chunks, 6), dma(chunks, 6), dma(chunks, 6), dma(chunks, 6),
        ],
        1,
    )(head_slopes, *given, w_qkv, w_out, w_up, w_down)

    return local(final_kernel, (shape(here, width), shape(here, width)), [VMEM] * 2)(
        back.reshape(owners, 16, 128), rows
    )


def solution(mesh):
    return jax.shard_map(
        on_device,
        mesh=mesh,
        in_specs=(
            P("flow", "tp"),
            P("flow"),
            P("flow"),
            P(),
            P(),
            P(None, None, "tp"),
            P("tp", None),
            P(None, "tp"),
            P("tp", None),
            P("tp"),
            P("tp"),
            P("tp"),
        ),
        out_specs=(P("flow", "tp"), P("flow", "tp")),
        check_vma=False,
    )
```

```python
import functools

import jax
import jax.numpy as jnp
from jax import lax
from jax.experimental import pallas as pl
from jax.experimental.pallas import tpu as pltpu
from jax.sharding import PartitionSpec as P

MESH = pl.DeviceIdType.MESH
F32, BF16 = jnp.float32, jnp.bfloat16
D = 1024
BLOCK = 128
KEEP = 5
HEAD_ROWS = 16
HEAD_DIM = 64
EPS = 1e-05
DIGIT = 128
LOG2E = 1.4426950408889634
FAR = 1e30
TALL = 160
VMEM_LIMIT = 56 * 1024 * 1024
VMEM = pl.BlockSpec(memory_space=pltpu.VMEM)
SMEM = pl.BlockSpec(memory_space=pltpu.SMEM)
HBM = pl.BlockSpec(memory_space=pltpu.HBM)


def iota(shape, dim):
    return lax.broadcasted_iota(jnp.int32, shape, dim)


def to_row(column):
    n = column.shape[0]
    eye = iota((n, n), 0) == iota((n, n), 1)
    return jnp.sum(jnp.where(eye, column, 0.0), axis=0, keepdims=True)


def to_column(row):
    n = row.shape[1]
    eye = iota((n, n), 0) == iota((n, n), 1)
    return jnp.sum(jnp.where(eye, row, 0.0), axis=1, keepdims=True)


def onehot(mask):
    return jnp.where(mask, 1.0, 0.0).astype(BF16)


def to_blocks(left, right):
    n = left.shape[0] // 8
    return jnp.concatenate([left.reshape(n, 8, 128), right.reshape(n, 8, 128)], axis=1).astype(BF16)


def from_blocks(blocks):
    n = blocks.shape[0]
    wide = blocks.astype(F32)
    return wide[:, :8].reshape(n * 8, 128).astype(BF16), wide[:, 8:].reshape(n * 8, 128).astype(BF16)


def norm_parts(parts, gains):
    total = sum(jnp.sum(p, axis=1, keepdims=True) for p in parts)
    square = sum(jnp.sum(p * p, axis=1, keepdims=True) for p in parts)
    mean = total / D
    scale = lax.rsqrt(square / D - mean * mean + EPS)
    return [((p - mean) * scale * g).astype(BF16) for p, g in zip(parts, gains)]


def final_kernel(in_ref, rows_ref, enc_ref, ctx_ref):
    given = jnp.concatenate(from_blocks(in_ref[...]), axis=1)
    at = iota((rows_ref.shape[0], given.shape[0]), 1).astype(F32)
    for column, out in ((0, enc_ref), (1, ctx_ref)):
        pick = onehot(at == rows_ref[:, column : column + 1])
        out[...] = jnp.dot(pick, given, preferred_element_type=F32).astype(BF16)


class Spot:
    def __init__(self, side):
        self.side = side
        flow = lax.axis_index("flow")
        self.tp = lax.axis_index("tp")
        self.core = lax.rem(flow, 2)
        chip = lax.div(flow, 2)
        self.y = lax.div(chip, side)
        self.z = lax.rem(chip, side)

    def seen(self, core):
        first = core == 0
        return jnp.where(first, self.y, self.z), jnp.where(first, self.z, self.y)

    def device(self, core, a, b, target_core):
        first = core == 0
        a, b = lax.rem(a + self.side, self.side), lax.rem(b + self.side, self.side)
        y, z = jnp.where(first, a, b), jnp.where(first, b, a)
        return ((y * self.side + z) * 2 + target_core, self.tp)

    def beside(self, step):
        parts = lax.axis_size("tp")
        return (lax.axis_index("flow"), lax.rem(self.tp + step + parts, parts))


def remote(src, dst, send, recv, device):
    return pltpu.make_async_remote_copy(
        src_ref=src, dst_ref=dst, send_sem=send, recv_sem=recv, device_id=device, device_id_type=MESH
    )


def started(copy):
    copy.start()
    return copy


class Ring:
    def __init__(self, spot, src, out, send, recv, cut, start=0, rows=None):
        self.me = spot.tp
        self.right, self.left = spot.beside(1), spot.beside(-1)
        self.src, self.out, self.send, self.recv = src, out, send, recv
        rows = src.shape[0] if rows is None else rows
        self.upper, self.lower = pl.ds(start, cut), pl.ds(start + cut, rows - cut)
        parts = lax.axis_size("tp")
        self.before = lax.rem(self.me + parts - 1, parts)
        self.after = lax.rem(self.me + 1, parts)
        self.far = lax.rem(self.me + 2, parts)

    def copy(self, i, block, part, device, own=False):
        src = self.src.at[part] if own and self.src is not None else self.out.at[block, part]
        return remote(src, self.out.at[block, part], self.send.at[i], self.recv.at[i], device)

    def start(self):
        self.first = [
            self.copy(0, self.me, self.upper, self.right, True),
            self.copy(1, self.me, self.lower, self.left, True),
            self.copy(2, self.me, self.lower, self.right, True),
            self.copy(3, self.me, self.upper, self.left, True),
        ]
        for copy in self.first:
            copy.start()

    def forward(self):
        self.copy(0, self.before, self.upper, self.right).wait_recv()
        self.up = self.copy(4, self.before, self.upper, self.right)
        self.up.start()
        self.copy(1, self.after, self.lower, self.left).wait_recv()
        self.down = self.copy(5, self.after, self.lower, self.left)
        self.down.start()

    def finish(self):
        self.copy(2, self.before, self.lower, self.right).wait_recv()
        self.copy(3, self.after, self.upper, self.left).wait_recv()
        self.copy(4, self.far, self.upper, self.right).wait_recv()
        self.copy(5, self.far, self.lower, self.left).wait_recv()
        for copy in (*self.first, self.up, self.down):
            copy.wait_send()


class Sum:
    def __init__(self, spot, terms, relay, pair, one, send, recv, start, rows):
        parts = lax.axis_size("tp")
        self.me = spot.tp
        self.right, self.left = spot.beside(1), spot.beside(-1)
        self.after, self.before, self.far = (lax.rem(self.me + i, parts) for i in (1, parts - 1, 2))
        self.terms, self.relay, self.pair, self.one = terms, relay, pair, one
        self.send, self.recv = send, recv
        self.upper, self.lower = pl.ds(start, rows // 2), pl.ds(start + rows // 2, rows // 2)

    def copy(self, i, src, dst, device):
        copy = remote(src, dst, self.send.at[i], self.recv.at[i], device)
        copy.start()
        return copy

    def start(self):
        terms = self.terms
        self.copies = [
            self.copy(0, terms.at[self.far, self.upper], self.relay.at[0], self.right),
            self.copy(1, terms.at[self.far, self.lower], self.relay.at[1], self.left),
            self.copy(2, terms.at[self.after, self.lower], self.one.at[1], self.right),
            self.copy(3, terms.at[self.before, self.upper], self.one.at[0], self.left),
        ]

    def forward(self):
        for i, (to, rows, device) in enumerate(
            ((self.after, self.upper, self.right), (self.before, self.lower, self.left))
        ):
            self.copies[i].wait_recv()
            self.relay[i] = (self.relay[i].astype(F32) + self.terms[to, rows, :].astype(F32)).astype(BF16)
            self.copies.append(self.copy(4 + i, self.relay.at[i], self.pair.at[i], device))

    def finish(self, keep, out):
        for i in range(2, 6):
            self.copies[i].wait_recv()
        for i, rows in ((0, self.upper), (1, self.lower)):
            terms = self.terms[self.me, rows, :].astype(F32) + self.pair[i].astype(F32) + self.one[i].astype(F32)
            out[rows, :] = (keep[self.me, rows, :].astype(F32) + terms).astype(BF16)
        for copy in self.copies:
            copy.wait_send()


def pack(spot, packets, flow_row, pos_row, holder, first_block):
    side = spot.side
    a, b = spot.seen(spot.core)
    here, flows = packets.shape[0], holder.shape[1]
    rows = 2 * side * side * 8
    flow = to_column(flow_row)
    pos = to_column(pos_row)
    pick = flow == iota((here, flows), 1).astype(F32)
    dest = jnp.sum(jnp.where(pick, holder, 0.0), axis=1, keepdims=True)
    first = jnp.sum(jnp.where(pick, first_block, 0.0), axis=1, keepdims=True)
    code = first * BLOCK + pos + 1.0
    high = jnp.floor(code * (1.0 / DIGIT))
    low = code - high * DIGIT
    before = (dest == to_row(dest)) & (iota((here, here), 0) > iota((here, here), 1))
    rank = jnp.sum(jnp.where(before, 1.0, 0.0), axis=1, keepdims=True)
    chip = jnp.floor(dest * 0.5)
    half = dest - 2.0 * chip
    major = jnp.floor((chip + 0.5) * (1.0 / side))
    minor = chip - major * side
    swap = spot.core == 1

    def ahead(value, mine):
        value = value - mine.astype(F32)
        return jnp.where(value < 0.0, value + side, value)

    a_off = ahead(jnp.where(swap, minor, major), a)
    b_off = ahead(jnp.where(swap, major, minor), b)
    c_off = jnp.abs(half - spot.core.astype(F32))
    base = ((a_off * side + b_off) * 2.0 + c_off) * 8.0
    odd = b_off - 2.0 * jnp.floor(b_off * 0.5)
    spread = (odd * side + a_off) * 8.0 + rank
    base_row, rank_row = to_row(base), to_row(rank)
    sub = iota((rows, here), 0).astype(F32)
    take = onehot(sub == base_row + rank_row)
    take_high = onehot(sub == base_row + 5.0)
    take_low = onehot(sub == base_row + 6.0)
    mine = iota((here, 128), 1).astype(F32) == spread
    left = (
        jnp.dot(take, packets[:, :128], preferred_element_type=F32)
        + jnp.dot(take_high, jnp.where(mine, high, 0.0).astype(BF16), preferred_element_type=F32)
        + jnp.dot(take_low, jnp.where(mine, low, 0.0).astype(BF16), preferred_element_type=F32)
    )
    right = jnp.dot(take, packets[:, 128:], preferred_element_type=F32)
    at = iota((here, 128), 1)
    pool = base + 5.0 + jnp.where(first > 0.0, 1.0, 0.0)
    return to_blocks(left, right), jnp.where(at == 0, base + rank, pool)


def squeeze(rows, padded, turned=False):
    dims = (padded, rows) if turned else (rows, padded)
    row = iota(dims, 1 if turned else 0).astype(F32)
    place = row + (8 - KEEP) * jnp.floor((row + 0.5) * (1.0 / KEEP))
    return onehot(iota(dims, 0 if turned else 1).astype(F32) == place)


def digits(left):
    rows = left.shape[0]
    groups = rows // 128
    r, g = iota((8, rows), 1), iota((8, rows), 0)
    out = []
    for row in (5, 6):
        pick = onehot((r >= g * 128) & (r < g * 128 + 128) & ((r & 7) == row))
        found = jnp.dot(pick, left, preferred_element_type=F32)
        out.append(jnp.concatenate([found[i : i + 1] for i in range(groups)], axis=1))
    return out


def layer_kernel(
    side, slope_ref, pk_any, flow_any, pos_any, holder_any, first_any, gain1_any, gain2_any,
    wq_any, wo_any, up_any, down_any, back_ref, rows_ref,
    pk_ref, flow_ref, pos_ref, holder_ref, first_ref, gain1_ref, gain2_ref, wq_ref, up_ref, down_ref, wo_ref,
    out_box, mid_ref, in_box, rep_ref, mid2_ref,
    all_ref, qkv_ref, far_ref, att_ref, keep_ref, terms_ref, enc_ref, relay, pair, one,
    lsem, s1, r1, s2, r2, s3, r3, s4, r4, wsend, wrecv, asend, arecv, gsend, grecv, ssend, srecv,
):
    spot = Spot(side)
    core, me = spot.core, spot.tp
    other = 1 - core
    a, b = spot.seen(core)
    oa, ob = spot.seen(other)
    rounds, few = 2, side // 2
    far_first = sorted(range(1, side), key=lambda i: -min(i, side - i))

    barrier = pltpu.get_barrier_semaphore()
    friends = [spot.beside(1), spot.beside(-1), spot.device(core, a, b, other)]
    for i in range(1, side):
        friends += [
            spot.device(core, a + i, b, core), spot.device(core, a, b + i, core),
            spot.device(core, a, b + i, other), spot.device(other, oa, ob + i, other),
        ]
    sources = (pk_any, flow_any, pos_any, holder_any, first_any, gain1_any, gain2_any, wq_any, up_any, down_any)
    holds = (pk_ref, flow_ref, pos_ref, holder_ref, first_ref, gain1_ref, gain2_ref, wq_ref, up_ref, down_ref)
    loads = [pltpu.make_async_copy(x, h, lsem.at[i]) for i, (x, h) in enumerate(zip(sources, holds))]
    share = wo_any.shape[0] // 2
    begin = pl.multiple_of(core * share, share)
    our = pl.ds(begin, share)
    loads.append(pltpu.make_async_copy(wo_any.at[our], wo_ref.at[me, our], lsem.at[len(loads)]))
    for load in loads[:7]:
        load.start()
    for device in friends:
        pl.semaphore_signal(barrier, inc=1, device_id=device, device_id_type=MESH)
    for load in loads[7:]:
        load.start()
    for load in loads[:7]:
        load.wait()
    flow_row, pos_row, holder, first_block = (
        ref[...].astype(F32)[None] for ref in (flow_ref, pos_ref, holder_ref, first_ref)
    )
    mine = holder == lax.axis_index("flow").astype(F32)
    edge = jnp.max(jnp.where(mine, first_block, 0.0), axis=1, keepdims=True) * BLOCK
    blocks, found = pack(spot, pk_ref[...], flow_row, pos_row, holder, first_block)
    out_box[...] = blocks.reshape(out_box.shape)
    rows_ref[...] = found
    parts, width = all_ref.shape[0], all_ref.shape[2]
    gain_rows = jnp.where(
        iota((HEAD_ROWS, width), 0) == 0, gain1_ref[...].astype(F32)[None], gain2_ref[...].astype(F32)[None]
    ).astype(BF16)
    all_ref[me, :HEAD_ROWS, :] = gain_rows
    pl.semaphore_wait(barrier, len(friends))

    def hop1(h):
        some = pl.ds(h * few, few)
        return [
            started(
                remote(out_box.at[i, some], mid_ref.at[i, some], s1.at[h, i], r1.at[h, i],
                       spot.device(core, a + i, b, core))
            )
            for i in far_first
        ]

    def hop2(h):
        return [
            started(
                remote(mid_ref.at[:, h * few + i, t], in_box.at[h, t, i], s2.at[h, i, t], r2.at[h, i, t],
                       spot.device(core, a, b + h * few + i, core if t == 0 else other))
            )
            for i in (range(few) if h else reversed(range(few))) for t in range(2) if h or i or t
        ]

    first = [hop1(0), hop1(1)]
    weights = Ring(spot, wo_any, wo_ref, wsend, wrecv, share // 2, begin, share)
    weights.start()
    mid_ref[0] = out_box[0]
    for copy in first[0]:
        copy.wait_recv()
    second = [hop2(0)]
    in_box[0, 0, 0] = mid_ref[:, 0, 0]
    weights.forward()
    for copy in first[1]:
        copy.wait_recv()
    second.append(hop2(1))
    weights.finish()
    loads[10].wait()
    swap = started(
        remote(wo_ref.at[:, our], wo_ref.at[:, our], wsend.at[6], wrecv.at[6], spot.device(core, a, b, other))
    )

    sources_here = side * side
    rows = sources_here * KEEP
    total = rounds * rows
    rings, high, low = [], [], []
    for h in range(rounds):
        for copy in second[h]:
            copy.wait_recv()
        left, right = from_blocks(in_box[h].reshape(sources_here, 16, 128))
        keep = squeeze(rows, sources_here * 8)
        here = pl.ds(HEAD_ROWS + h * rows, rows)
        all_ref[me, here, :128] = jnp.dot(keep, left, preferred_element_type=F32).astype(BF16)
        all_ref[me, here, 128:] = jnp.dot(keep, right, preferred_element_type=F32).astype(BF16)
        begin = HEAD_ROWS * (h > 0) + h * rows
        rings.append(
            Ring(spot, None, all_ref, asend.at[h], arecv.at[h], rows // 2, begin, rows + HEAD_ROWS * (h == 0))
        )
        rings[h].start()
        found = digits(left)
        high.append(found[0])
        low.append(found[1])
    both = jnp.where(
        iota((8, total // KEEP * 8), 0) == 0, jnp.concatenate(high, axis=1), jnp.concatenate(low, axis=1)
    ).astype(BF16)
    keep = squeeze(total, total // KEEP * 8)
    across = (((1,), (1,)), ((), ()))
    by_row = lax.dot_general(both, keep, across, preferred_element_type=F32)
    by_column = lax.dot_general(keep, both, across, preferred_element_type=F32)
    slot_row = by_row[0:1] * DIGIT + by_row[1:2] - 1.0
    slot_column = by_column[:, 0:1] * DIGIT + by_column[:, 1:2] - 1.0
    tag_row = jnp.where(slot_row >= edge, 1.0, 0.0)
    tag_column = jnp.where(slot_column >= edge, 1.0, 0.0)

    rings[0].forward()
    loads[7].wait()
    gains = None
    for h in range(rounds):
        if h + 1 < rounds:
            rings[h + 1].forward()
        rings[h].finish()
        if gains is None:
            gains = [all_ref[p, :HEAD_ROWS, :].astype(F32) for p in range(parts)]
        here = pl.ds(HEAD_ROWS + h * rows, rows)
        normed = jnp.concatenate(
            norm_parts([all_ref[p, here, :].astype(F32) for p in range(parts)], [g[0:1] for g in gains]), axis=1
        )
        for k in range(3):
            qkv_ref[k, pl.ds(h * rows, rows), :] = jnp.dot(normed, wq_ref[k], preferred_element_type=F32).astype(BF16)

    number = iota((8, total), 0).astype(F32)
    members = jnp.where((slot_row >= 0.0) & (tag_row == number), 1.0, 0.0)
    counts = jnp.sum(members, axis=1, keepdims=True)

    def attend(chunk):
        rows = pl.ds(chunk * TALL, TALL)
        part = slice(chunk * TALL, (chunk + 1) * TALL)
        itself = iota((TALL, total), 0) + chunk * TALL == iota((TALL, total), 1)
        allowed = ((tag_column[part] == tag_row) & (slot_row >= 0.0)) | itself
        far_ref[...] = jnp.where(allowed, jnp.abs(slot_column[part] - slot_row) * LOG2E, FAR)
        first = iota((TALL, 128), 1) < HEAD_DIM
        for two in range(width // 128):
            cols = slice(two * 128, (two + 1) * 128)
            query = qkv_ref[0, rows, cols]
            keys, values = qkv_ref[1, :, cols], qkv_ref[2, :, cols]
            halves = []
            for half in range(2):
                mine = jnp.where(first == (half == 0), query, jnp.zeros_like(query))
                scores = lax.dot_general(mine, keys, across, preferred_element_type=F32)
                weights = jnp.exp2(
                    scores * (HEAD_DIM**-0.5 * LOG2E) - slope_ref[2 * two + half] * far_ref[...]
                )
                probs = weights * (1.0 / jnp.sum(weights, axis=1, keepdims=True))
                halves.append(jnp.dot(probs.astype(BF16), values, preferred_element_type=F32))
            att_ref[me, rows, cols] = jnp.where(first, halves[0], halves[1]).astype(BF16)

    def forward_layer(chunk):
        rows = pl.ds(chunk * TALL, TALL)
        there = pl.ds(HEAD_ROWS + chunk * TALL, TALL)
        attn = sum(
            jnp.dot(att_ref[p, rows, :], wo_ref[p], preferred_element_type=F32).astype(BF16).astype(F32)
            for p in range(parts)
        )
        middle = [
            (all_ref[p, there, :].astype(F32) + attn[:, p * width : (p + 1) * width]).astype(BF16)
            for p in range(parts)
        ]
        for p in range(parts):
            keep_ref[p, rows, :] = middle[p]
        normed = jnp.concatenate(norm_parts([m.astype(F32) for m in middle], [g[1:2] for g in gains]), axis=1)
        upward = jnp.dot(normed, up_ref[...], preferred_element_type=F32)
        active = (0.5 * upward * (1.0 + lax.erf(upward * (0.5**0.5)))).astype(BF16)
        for p in range(parts):
            terms_ref[p, rows, :] = jnp.dot(
                active, down_ref[:, p * width : (p + 1) * width], preferred_element_type=F32
            ).astype(BF16)

    chunks = total // TALL
    rings = [Ring(spot, None, att_ref, gsend.at[c], grecv.at[c], TALL // 2, c * TALL, TALL) for c in range(chunks)]
    sums = [
        Sum(spot, terms_ref, relay.at[c], pair.at[c], one.at[c], ssend.at[c], srecv.at[c], c * TALL, TALL)
        for c in range(chunks)
    ]
    for c in range(chunks):
        attend(c)
        rings[c].start()
        if c:
            rings[c - 1].forward()
    theirs = pl.ds(pl.multiple_of(other * share, share), share)
    remote(
        wo_ref.at[:, theirs], wo_ref.at[:, theirs], wsend.at[6], wrecv.at[6], spot.device(core, a, b, other)
    ).wait_recv()
    for load in loads[8:10]:
        load.wait()
    for c in range(chunks):
        if c == 1:
            rings[chunks - 1].forward()
        rings[c].finish()
        forward_layer(c)
        sums[c].start()
        if c:
            sums[c - 1].forward()
    expand = squeeze(TALL, TALL // KEEP * 8, True)

    def settle(c):
        sums[c].finish(keep_ref, enc_ref)
        wide = jnp.dot(expand, enc_ref[pl.ds(c * TALL, TALL), :], preferred_element_type=F32)
        rep_ref[c // 2, c % 2] = to_blocks(wide[:, :128], wide[:, 128:]).reshape(few, side, 16, 128)

    settle(0)
    settle(1)
    sums[chunks - 1].forward()
    settle(2)
    settle(3)

    pooled = jnp.dot(members.astype(BF16), enc_ref[...], preferred_element_type=F32) / counts
    line = iota((16, 128), 0)
    near = jnp.where(line < 8, pooled[0:1, :128], pooled[0:1, 128:])
    next_to = jnp.where(line < 8, pooled[1:2, :128], pooled[1:2, 128:])
    tile = jnp.where((line & 7) == 5, near, jnp.where((line & 7) == 6, next_to, 0.0)).astype(BF16)
    rep_ref[...] = rep_ref[...] + tile

    third, fourth = [[] for _ in range(rounds)], []
    for h in range(rounds):
        for i in range(few):
            for t in range(2):
                if h or i or t:
                    frame, fa, fb = (core, a, b) if t == 0 else (other, oa, ob)
                    far = h * few + i
                    third[h].append(
                        started(
                            remote(rep_ref.at[h, t, i], mid2_ref.at[:, far, t], s3.at[far, t], r3.at[far, t],
                                   spot.device(frame, fa, fb - far, frame))
                        )
                    )
    mid2_ref[:, 0, 0] = rep_ref[0, 0, 0]
    for h in range(rounds):
        for copy in third[h]:
            copy.wait_recv()
        some = pl.ds(h * few, few)
        for i in far_first:
            fourth.append(
                started(
                    remote(mid2_ref.at[i, some], back_ref.at[i, some], s4.at[h, i], r4.at[h, i],
                           spot.device(core, a - i, b, core))
                )
            )
        back_ref[0, some] = mid2_ref[0, some]
    for copy in fourth:
        copy.wait_recv()
    for copy in (*first[0], *first[1], *second[0], *second[1], *third[0], *third[1], *fourth, swap):
        copy.wait_send()


def shape(*dims, dtype=BF16):
    return jax.ShapeDtypeStruct(dims, dtype)


def local(kernel, outs, specs, scratch=()):
    return pl.pallas_call(
        kernel,
        out_shape=outs,
        in_specs=specs,
        out_specs=jax.tree.map(lambda _: VMEM, outs),
        scratch_shapes=list(scratch),
        compiler_params=pltpu.CompilerParams(vmem_limit_bytes=VMEM_LIMIT),
    )


def linked(kernel, outs, inputs, scratch, number):
    return pl.pallas_call(
        kernel,
        out_shape=outs,
        in_specs=[VMEM] * inputs if isinstance(inputs, int) else inputs,
        out_specs=jax.tree.map(lambda _: VMEM, outs),
        scratch_shapes=scratch,
        compiler_params=pltpu.CompilerParams(
            vmem_limit_bytes=VMEM_LIMIT, collective_id=number, has_side_effects=True
        ),
    )


def dma(*dims):
    return pltpu.SemaphoreType.DMA(dims)


def on_device(
    packets, packet_flow, packet_pos, flow_holder_rank, flow_first_block,
    w_qkv, w_out, w_up, w_down, gain_first, gain_second, head_slopes,
):
    owners, parts = lax.axis_size("flow"), lax.axis_size("tp")
    side = int(round((owners // 2) ** 0.5))
    here, width = packets.shape
    total = owners * KEEP
    chunks = total // TALL
    given = (packets, packet_flow, packet_pos, flow_holder_rank, flow_first_block, gain_first, gain_second)
    box, turned = (side, side, 2, 16, 128), (2, 2, side // 2, side, 16, 128)

    def hold(*dims):
        return pltpu.VMEM(dims, BF16)

    some = hold(chunks, 2, TALL // 2, width)
    full = hold(parts, total, width)
    back, rows = linked(
        functools.partial(layer_kernel, side),
        (shape(*box), shape(here, 128, dtype=F32)),
        [SMEM] + [HBM] * 11,
        [
            *(pltpu.VMEM(v.shape, v.dtype) for v in (*given, w_qkv, w_up, w_down)), hold(parts, *w_out.shape),
            hold(*box), hold(*box), hold(*turned), hold(*turned), hold(*box),
            hold(parts, HEAD_ROWS + total, width), hold(3, total, width), pltpu.VMEM((TALL, total), F32),
            full, full, full, hold(total, width), some, some, some,
            dma(11), dma(2, side), dma(2, side), dma(2, side // 2, 2), dma(2, side // 2, 2),
            dma(side, 2), dma(side, 2), dma(2, side), dma(2, side), dma(7), dma(7), dma(2, 6), dma(2, 6),
            dma(chunks, 6), dma(chunks, 6), dma(chunks, 6), dma(chunks, 6),
        ],
        1,
    )(head_slopes, *given, w_qkv, w_out, w_up, w_down)

    return local(final_kernel, (shape(here, width), shape(here, width)), [VMEM] * 2)(
        back.reshape(owners, 16, 128), rows
    )


def solution(mesh):
    return jax.shard_map(
        on_device,
        mesh=mesh,
        in_specs=(
            P("flow", "tp"),
            P("flow"),
            P("flow"),
            P(),
            P(),
            P(None, None, "tp"),
            P("tp", None),
            P(None, "tp"),
            P("tp", None),
            P("tp"),
            P("tp"),
            P("tp"),
        ),
        out_specs=(P("flow", "tp"), P("flow", "tp")),
        check_vma=False,
    )
```
